512 devices in a mesh: gx: 32 (over x_lo, y, core), gy: 16 (over z, x_hi).
Axes of the slice: x: 4 (x_hi: 2, x_lo: 2; x = x_hi * 2 + x_lo), y: 8, z: 8, core: 2. Of those that a mesh axis runs over, the one named last changes fastest.
Arguments:
- density: float32 [8192, 8192], P('gx', 'gy'), may hold values from 0.05 to 0.95
- kernel_hat: float32 [8192, 8192], P(('gx', 'gy')), may hold values from -18 to 18
Outputs:
- potential: float32 [8192, 8192], P('gx', 'gy')
- new_density: float32 [8192, 8192], P('gx', 'gy')
The draws below stay inside these ranges and needn't reach their ends.
All inputs are finite; a program needn't handle non-finite values.
Results may differ from the reference program's by a relative error of at most 0.00012.
Values sent between devices are 32-bit elements; how exact they have to be, the bound alone decides.
A program may use at most 64 MiB of HBM per device.

```python
import jax
import jax.numpy as jnp

NX = 8192
NY = 8192


def block_scale(own_key, shape, shards, low, high):
    factor_of, own = 1.0, jax.random.fold_in(own_key, 6)
    for dim, shards_of in shards:
        steps = jnp.exp(jax.random.uniform(jax.random.fold_in(own, dim), (shards_of,), jnp.float32, low / len(shards), high / len(shards)))
        factor_of = factor_of * jnp.repeat(steps, shape[dim] // shards_of).reshape([-1 if axis == dim else 1 for axis in range(len(shape))])
    return factor_of


def noise(own_key, dims, width, limit, pieces=(), dtype=jnp.bfloat16):
    loudness = block_scale(own_key, dims, pieces, -0.22, 0.18) if pieces else 1.0
    values = jax.random.normal(own_key, dims, jnp.float32) * width * loudness
    return jnp.minimum(jnp.maximum(values, -limit), limit).astype(dtype)


def setup_inputs(seed: int = 0) -> dict:
    streams_of = jax.random.split(jax.random.key(seed), 3)
    return {
        "density": jnp.clip(0.05 + 0.9 * jax.random.uniform(streams_of[0], (NX, NY), jnp.float32) ** block_scale(streams_of[0], (NX, NY), ((0, 32), (1, 16)), -0.2, 0.2), 0.05, 0.95),
        "kernel_hat": noise(streams_of[1], (NX, NY), 3.0, 18.0, ((0, 512),), jnp.float32),
    }


time_step = 0.2
diffusion_rate = 0.25


def face_flux(lower_rho, upper_rho, lower_pot, upper_pot):
    speed = lower_pot - upper_pot
    drift = jnp.maximum(speed, 0.0) * lower_rho * (1.0 - upper_rho) + jnp.minimum(speed, 0.0) * upper_rho * (1.0 - lower_rho)
    spread = diffusion_rate * (lower_rho * lower_rho - upper_rho * upper_rho)
    return drift + spread


def reference(density, kernel_hat):
    spectrum = jnp.fft.fft2(density)
    filtered = spectrum * kernel_hat
    potential = jnp.real(jnp.fft.ifft2(filtered)).astype(jnp.float32)
    flux_first = face_flux(density, jnp.roll(density, -1, 0), potential, jnp.roll(potential, -1, 0))
    flux_second = face_flux(density, jnp.roll(density, -1, 1), potential, jnp.roll(potential, -1, 1))
    div_first = flux_first - jnp.roll(flux_first, 1, 0)
    div_second = flux_second - jnp.roll(flux_second, 1, 1)
    new_density = density - time_step * (div_first + div_second)
    return potential, new_density
```

```python
import functools

import jax
import jax.numpy as jnp
import numpy as np
from jax import lax
from jax.experimental import pallas as pl
from jax.experimental.pallas import tpu as pltpu
from jax.sharding import PartitionSpec as P

TIME_STEP = 0.2
DIFFUSION = 0.25
MESH = pl.DeviceIdType.MESH
F32, BF16 = jnp.float32, jnp.bfloat16
NGX, NGY, N = 32, 16, 8192
ROWS, COLS = 256, 512


def split_np(table):
    table = np.asarray(table, np.float32)
    high = table.astype(BF16)
    low = (table - high.astype(np.float32)).astype(BF16)
    return high, low


def angle(a, b, modulus):
    product = np.asarray(a, np.int64) * np.asarray(b, np.int64) % modulus
    return 2.0 * np.pi * product / modulus


def slot_frequency(half, side, j):
    if half == 0:
        return j + 1 if side == 0 else 16 - j
    return j if side == 0 else 15 - j


@functools.lru_cache(maxsize=None)
def tables():
    t = {}
    eye8 = np.eye(8)
    g = np.arange(32)
    slots = np.arange(16)
    real_rows = np.cos(angle(slots[:, None], g[None], 32))
    imag_rows = -np.sin(angle(slots[:, None], g[None], 32))
    imag_rows[0] = np.cos(angle(16, g, 32))
    t["first"] = split_np(np.kron(np.concatenate([real_rows, imag_rows]), eye8))
    m = np.arange(256)
    theta = angle(slots[:, None], m[None], N)
    last = angle(16, m, N)
    ca, sa, cb, sb = np.cos(theta), np.sin(theta), np.cos(theta), np.sin(theta)
    ca[0], sa[0], cb[0], sb[0] = 0.0, np.cos(last), -np.sin(last), 0.0
    t["twist_first"] = np.repeat(np.stack([ca, sa, cb, sb]), 8, axis=1).astype(np.float32)
    w256 = angle(m[:, None], m[None], 256)
    c256, s256 = np.cos(w256), np.sin(w256)
    forward = np.concatenate([c256, s256], axis=1)
    ones = np.zeros((16, 512))
    ones[0, :256] = 1.0
    t["second"] = split_np(np.concatenate([forward[:128], forward[128:], ones]))
    a = np.arange(512)
    w512 = angle(a[:, None], a[None], 512)
    t["c512"] = split_np(np.cos(w512))
    t["s512"] = split_np(np.sin(w512))
    lane = np.arange(256)
    l16 = 8 * (lane // 128) + lane % 8
    theta = angle(a[:, None], l16[None], N)
    t["twist_rows"] = np.stack([np.cos(theta), np.sin(theta)]).astype(np.float32)
    lin = np.arange(16)
    phi = angle(lin[:, None], lin[None], 16)

    def embed(sign):
        out = np.zeros((2, 2, 8, 8, 2, 16, 8))
        for c in range(2):
            for l8 in range(8):
                co, si = np.cos(phi[8 * c + l8]), sign * np.sin(phi[8 * c + l8])
                for j in range(8):
                    out[c, 0, j, l8, 0, :, j] = co
                    out[c, 0, j, l8, 1, :, j] = si
                    out[c, 1, j, l8, 0, :, j] = -si
                    out[c, 1, j, l8, 1, :, j] = co
        return out.reshape(256, 256)

    def times_i_rows(matrix):
        parts = matrix.reshape(2, 2, 64, -1)
        return np.stack([parts[:, 1], -parts[:, 0]], axis=1).reshape(matrix.shape)

    m2 = embed(-1.0)
    t["sixteen"] = split_np(np.concatenate([m2, times_i_rows(m2)]))
    back = embed(1.0).reshape(2, 2, 8, 8, 2, 16, 8).transpose(4, 5, 6, 0, 1, 2, 3)
    inv = np.zeros((2, 16, 8, 2, 2, 8, 8))
    for c in range(2):
        for l8 in range(8):
            co, si = np.cos(phi[8 * c + l8]), np.sin(phi[8 * c + l8])
            for j in range(8):
                inv[0, :, j, c, 0, j, l8] = co
                inv[0, :, j, c, 1, j, l8] = si
                inv[1, :, j, c, 0, j, l8] = -si
                inv[1, :, j, c, 1, j, l8] = co
    del back
    turned = np.zeros_like(inv)
    turned[:, :, :, :, 0] = -inv[:, :, :, :, 1]
    turned[:, :, :, :, 1] = inv[:, :, :, :, 0]
    t["sixteen_back"] = split_np(np.concatenate([inv.reshape(256, 256), turned.reshape(256, 256)], axis=1))
    t["second_back"] = split_np(
        np.concatenate([np.concatenate([c256[:, h], s256[:, h]]) for h in (slice(0, 128), slice(128, 256))])
    )
    freq = np.zeros((2, 2, 2, 8, 8), np.int64)
    for half in range(2):
        for side in range(2):
            for j in range(8):
                freq[half, side, :, j, :] = slot_frequency(half, side, j)
    flat = freq.reshape(2, 256)
    theta = angle(m[None, :, None], flat[:, None, :], N)
    t["twist_last"] = np.stack([np.cos(theta), np.sin(theta)], axis=1).reshape(4, 256, 256).astype(np.float32)
    last = np.zeros((32, 8, 2, 2, 2, 2, 8, 8))
    scale = 2.0 / (float(N) * float(N))
    for half in range(2):
        for side in range(2):
            conj = 1.0 if side == 0 else -1.0
            for j in range(8):
                arc = angle(g, slot_frequency(half, side, j), 32)
                for l in range(8):
                    last[:, l, half, 0, side, 0, j, l] = scale * np.cos(arc)
                    last[:, l, half, 0, side, 1, j, l] = -scale * np.sin(arc) * conj
                    last[:, l, half, 1, side, 0, j, l] = -scale * np.sin(arc)
                    last[:, l, half, 1, side, 1, j, l] = -scale * np.cos(arc) * conj
    t["last"] = split_np(last.reshape(256, 1024))
    flip = np.zeros((512, 512))
    flip[a, (-a) % 512] = 1.0
    t["flip"] = flip.astype(BF16)
    order = np.zeros((2, 16, 8, 16, 8))
    for kb in range(16):
        for s in range(8):
            order[0, kb, s, kb, 7 - s] = 1.0
            order[1, kb, s, kb, (8 - s) % 8] = 1.0
    t["order"] = order.reshape(2, 128, 128).astype(BF16)
    return t


def split(x):
    high = x.astype(BF16)
    return high, (x - high.astype(F32)).astype(BF16)


def mul(a, b, transposed=False):
    dims = (((1,), (1 if transposed else 0,)), ((), ()))
    dot = lambda x, y: lax.dot_general(x, y, dims, preferred_element_type=F32)
    return dot(a[0], b[0]) + (dot(a[0], b[1]) + dot(a[1], b[0]))


def mul_exact(selector, x, transposed=False):
    dims = (((1,), (1 if transposed else 0,)), ((), ()))
    dot = lambda p, q: lax.dot_general(p, q, dims, preferred_element_type=F32)
    high, low = split(x)
    return dot(selector, high) + dot(selector, low)


def first_forward(x, first, twist, second):
    spun = mul(first, split(x))
    real, imag = spun[:128], spun[128:]
    plain = real[:8]
    turned_real = real * twist[0] + imag * twist[1]
    turned_imag = imag * twist[2] - real * twist[3]

    def rows(table, order):
        return [table[8 * s : 8 * s + 8] for s in order]

    outs = []
    for half in range(2):
        if half == 0:
            near, far = list(range(1, 9)), [0] + list(range(15, 8, -1))
            re, im = turned_real, turned_imag
        else:
            near, far = list(range(8)), list(range(15, 7, -1))
            re = jnp.concatenate([plain, turned_real[8:]], axis=0)
            im = jnp.concatenate([jnp.zeros_like(plain), turned_imag[8:]], axis=0)
        cosine = jnp.concatenate(rows(re, near) + rows(im, near) + rows(re, far) + rows(-im, far), axis=0)
        sine = jnp.concatenate(rows(im, near) + rows(-re, near) + rows(im, far) + rows(re, far), axis=0)
        cosine, sine = split(cosine), split(sine)
        picked = slice(0, 128) if half == 0 else slice(128, 272)
        w = [v[picked] for v in second]
        out = mul([v[:, :256] for v in w], cosine, True) + mul([v[:, 256:] for v in w], sine, True)
        outs.append(out)
    low, high = outs[0], outs[1][:128]
    total = outs[1][128:136, :128]
    tile = high[:8, :128]
    row = lax.broadcasted_iota(jnp.int32, (8, 128), 0)
    lane = lax.broadcasted_iota(jnp.int32, (8, 128), 1)
    tile = jnp.where((row == 0) & (lane >= 64) & (lane < 72), pltpu.roll(tile, 64, 1), tile)
    tile = jnp.where((row == 0) & (lane < 8), total, tile)
    near_high = jnp.concatenate([tile, high[8:, :128]], axis=0)
    return low[:, :128], low[:, 128:], near_high, high[:, 128:]


def first_inverse(low, high, second_back, twist, last):
    row = lax.broadcasted_iota(jnp.int32, (8, 128), 0)
    lane = lax.broadcasted_iota(jnp.int32, (8, 128), 1)
    tile = high[:8, :128]
    constant = jnp.where(lane < 8, 0.5 * tile, 0.0)[:1]
    other = jnp.where(lane < 8, 0.5 * pltpu.roll(tile, 64, 1), jnp.where((lane >= 64) & (lane < 72), 0.0, tile))
    tile = jnp.where(row == 0, other, tile)
    top = jnp.concatenate([tile, high[:8, 128:]], axis=1)
    high = jnp.concatenate([top, high[8:]], axis=0)
    total = None
    for half, x in ((0, low), (1, high)):
        spun = mul([v[512 * half : 512 * half + 512] for v in second_back], split(x))
        cosine, sine = spun[:256], spun[256:]
        if half == 1:
            cosine = jnp.concatenate([cosine[:, :128] + constant, cosine[:, 128:]], axis=1)
        co, si = twist[2 * half], twist[2 * half + 1]
        one = co * cosine - si * sine
        two = si * cosine + co * sine
        for k, part in ((0, one), (1, two)):
            at = 512 * half + 256 * k
            term = mul([v[:, at : at + 256] for v in last], split(part), True)
            total = term if total is None else total + term
    return total


def face_flux(lower_rho, upper_rho, lower_pot, upper_pot):
    speed = lower_pot - upper_pot
    drift = jnp.maximum(speed, 0.0) * lower_rho * (1.0 - upper_rho) + jnp.minimum(speed, 0.0) * upper_rho * (
        1.0 - lower_rho
    )
    return drift + DIFFUSION * (lower_rho * lower_rho - upper_rho * upper_rho)


def weights_layout(own, other, flip, order):
    direct = jnp.concatenate([own[:, 512 * b : 512 * b + 512] for b in range(16)], axis=0)
    mirror = jnp.concatenate([other[:, 512 * (15 - b) : 512 * (15 - b) + 512] for b in range(16)], axis=0)
    turned = mul_exact(flip, mirror, True)
    top = turned[:8]
    row = lax.broadcasted_iota(jnp.int32, (8, 128), 0)
    top = jnp.where(row == 0, pltpu.roll(top, 8, 1), top)
    turned = jnp.concatenate([top, turned[8:]], axis=0)
    high, low = split(turned)
    turned = jnp.dot(high, order, preferred_element_type=F32) + jnp.dot(low, order, preferred_element_type=F32)
    return 0.5 * (direct.T + turned)


CONSTANTS = (
    "first", "twist_first", "second", "c512", "s512", "twist_rows", "sixteen", "sixteen_back",
    "second_back", "twist_last", "last", "flip", "order",
)


def flat_constants():
    out, index = [], {}
    for name in CONSTANTS:
        value = tables()[name]
        value = value if isinstance(value, tuple) else (value,)
        index[name] = list(range(len(out), len(out) + len(value)))
        out.extend(value)
    return out, index


def kernel(index, n_const, *refs):
    rho_ref, kernel_ref = refs[:2]
    const_hbm = refs[2 : 2 + n_const]
    pot_ref, new_ref = refs[2 + n_const : 4 + n_const]
    rest = list(refs[4 + n_const :])
    const = [rest.pop(0) for _ in range(n_const)]
    (
        rho, weights, weights_got, row0_send, row0_got, wk, wk2,
        send1, recv1, send2, recv2, send3, recv3, send4, recv4, send5, recv5, send6, recv6,
        spread, edge_rows, edge_cols, halo_rows, halo_cols, padded_rho, padded_pot,
        send_sem, recv_sem, local_sem, const_sem, k_send, k_recv, halo_send, halo_recv,
    ) = rest
    gx, gy = lax.axis_index("gx"), lax.axis_index("gy")
    device = gx * NGY + gy
    lower = device < 256

    def get(name):
        return [const[i] for i in index[name]]

    mirror = {"gx": NGX - 1 - gx, "gy": NGY - 1 - gy}
    other = jnp.where(device == 0, 256, jnp.where(device == 256, 0, 512 - device))
    row_partner = {"gx": other // NGY, "gy": lax.rem(other, NGY)}

    barrier = pltpu.get_barrier_semaphore()

    def greet(axis, n, me):
        def body(i, carry):
            pl.semaphore_signal(barrier, inc=1, device_id={axis: lax.rem(me + i, n)}, device_id_type=MESH)
            return carry

        lax.fori_loop(1, n, body, 0)

    greet("gx", NGX, gx)
    greet("gy", NGY, gy)
    pl.semaphore_signal(barrier, inc=1, device_id=mirror, device_id_type=MESH)
    pl.semaphore_signal(barrier, inc=1, device_id=row_partner, device_id_type=MESH)

    load_rho = pltpu.make_async_copy(rho_ref, rho, local_sem.at[0])
    load_weights = pltpu.make_async_copy(kernel_ref, weights, local_sem.at[1])
    load_rho.start()
    load_weights.start()
    loads = [pltpu.make_async_copy(const_hbm[i], const[i], const_sem.at[i]) for i in range(n_const)]
    for load in loads:
        load.start()

    def ready(*names):
        for name in names:
            for i in index[name]:
                loads[i].wait()

    load_rho.wait()
    for b in range(4):
        turned = rho[:, 128 * b : 128 * b + 128].T
        for part in range(8):
            for c in range(2):
                send1[c, 8 * b + part] = turned[16 * part + 8 * c : 16 * part + 8 * c + 8]
    edge_rows[0] = rho[0:1, :]
    edge_rows[1] = rho[ROWS - 1 : ROWS, :]
    edge_cols[0] = send1[0, 0, 0:1, :]
    edge_cols[1] = send1[1, NGX - 1, 7:8, :]
    load_weights.wait()
    row0_send[...] = weights[0:1, :]

    pl.semaphore_wait(barrier, NGX - 1 + NGY - 1 + 2)

    def message(phase, c, i, axis, n, me, source, target):
        to = lax.rem(me + i, n)
        return pltpu.make_async_remote_copy(
            src_ref=source(to), dst_ref=target(to), send_sem=send_sem.at[phase, c, i],
            recv_sem=recv_sem.at[phase, c, i], device_id={axis: to}, device_id_type=MESH,
        )

    def start_phase(phase, c, axis, n, me, source, target):
        def body(i, carry):
            message(phase, c, i, axis, n, me, source, target).start()
            return carry

        own = pltpu.make_async_copy(source(me), target(me), local_sem.at[2 + 2 * phase + c])
        own.start()
        lax.fori_loop(1, n, body, 0)

    def finish_phase(phase, c, axis, n, me, source, target):
        def body(i, carry):
            message(phase, c, i, axis, n, me, source, target).wait_recv()
            return carry

        pltpu.make_async_copy(source(me), target(me), local_sem.at[2 + 2 * phase + c]).wait()
        lax.fori_loop(1, n, body, 0)

    def sent_phase(phase, c, axis, n, me, source, target):
        def body(i, carry):
            message(phase, c, i, axis, n, me, source, target).wait_send()
            return carry

        lax.fori_loop(1, n, body, 0)

    def slot_of(y):
        q, b = y // 2, lax.rem(y, 2)
        return b * 8 + jnp.where(b == 0, q, 7 - q)

    def at(ref, c, start, size):
        return ref.at[c, pl.ds(pl.multiple_of(start, size), size)]

    def phase(p, c):
        if p == 0:
            return p, c, "gx", NGX, gx, lambda to: send1.at[c, to], lambda to: recv1.at[c, gx]
        if p == 1:
            return p, c, "gx", NGX, gx, lambda to: at(send2, c, to * 16, 16), lambda to: at(recv2, c, gx * 16, 16)
        if p == 2:
            return (
                p, c, "gy", NGY, gy,
                lambda to: send3.at[c, slot_of(to)],
                lambda to: at(recv3, c, gy * 32, 32),
            )
        if p == 3:
            return (
                p, c, "gy", NGY, gy,
                lambda to: at(send4, c, to * 32, 32),
                lambda to: at(recv4, c, slot_of(gy) * 32, 32),
            )
        if p == 4:
            return p, c, "gx", NGX, gx, lambda to: at(send5, c, to * 16, 16), lambda to: at(recv5, c, gx * 16, 16)
        return (
            p, c, "gx", NGX, gx,
            lambda to: at(send6, c, to * 8, 8),
            lambda to: recv6.at[pl.ds(pl.multiple_of(gx * 16 + 8 * c, 8), 8)],
        )

    def halo(which, kind, source, k):
        axis, n, me = (("gx", NGX, gx), ("gy", NGY, gy))[kind]
        to = lax.rem(me + (n - 1 if k == 0 else 1), n)
        target = halo_rows if kind == 0 else halo_cols
        return pltpu.make_async_remote_copy(
            src_ref=source.at[2 * which + k], dst_ref=target.at[2 * which + k],
            send_sem=halo_send.at[4 * which + 2 * kind + k], recv_sem=halo_recv.at[4 * which + 2 * kind + k],
            device_id={axis: to}, device_id_type=MESH,
        )

    def halos(which):
        return [halo(which, kind, src, k) for kind, src in ((0, edge_rows), (1, edge_cols)) for k in range(2)]

    weights_copy = pltpu.make_async_remote_copy(
        src_ref=weights.at[pl.ds(8, 8)], dst_ref=weights_got, send_sem=k_send.at[0], recv_sem=k_recv.at[0],
        device_id=mirror, device_id_type=MESH,
    )
    row_copy = pltpu.make_async_remote_copy(
        src_ref=row0_send, dst_ref=row0_got, send_sem=k_send.at[1], recv_sem=k_recv.at[1],
        device_id=row_partner, device_id_type=MESH,
    )

    start_phase(*phase(0, 0))
    start_phase(*phase(0, 1))
    weights_copy.start()
    for copy in halos(0):
        copy.start()

    @pl.when(lower)
    def _():
        row_copy.start()

    ready("first", "twist_first", "second")
    first, second, twist_first = get("first"), get("second"), get("twist_first")[0]
    for c in range(2):
        finish_phase(*phase(0, c))
        x = recv1[c].reshape(256, 256)
        near_low, far_low, near_high, far_high = first_forward(
            x, [r[...] for r in first], twist_first, [r[...] for r in second]
        )
        for t in range(16):
            rows = slice(8 * t, 8 * t + 8)
            send2[c, 16 * t : 16 * t + 8] = near_low[rows]
            send2[c, 16 * (16 + t) : 16 * (16 + t) + 8] = near_high[rows]
            send2[c, 16 * (31 - t) + 8 : 16 * (31 - t) + 16] = far_low[rows]
            send2[c, 16 * (15 - t) + 8 : 16 * (15 - t) + 16] = far_high[rows]
        start_phase(*phase(1, c))

    ready("flip", "order")
    flip = get("flip")[0][...]
    order_ref = get("order")[0]
    order = jnp.where(lower, order_ref[0].astype(F32), order_ref[1].astype(F32)).astype(BF16)
    weights_copy.wait_recv()

    @pl.when(jnp.logical_not(lower))
    def _():
        row_copy.wait_recv()
        weights_got[0:1, :] = row0_got[...]

    own = jnp.where(lower, weights[1:9, :], weights[0:8, :])
    spread[...] = own

    @pl.when(device == 256)
    def _():
        one, two = spread[0:1, :], row0_got[...]
        half_difference = 0.5 * (one - two)
        row = lax.broadcasted_iota(jnp.int32, (8, N), 0)
        only = jnp.where(row == 0, jnp.broadcast_to(-half_difference, (8, N)), 0.0)
        wk2[...] = weights_layout(only, only, flip, order)
        half_sum = 0.5 * (one + two)
        spread[0:1, :] = half_sum
        weights_got[0:1, :] = half_sum

    wk[...] = weights_layout(spread[...], weights_got[...], flip, order)

    for c in range(2):
        finish_phase(*phase(1, c))
        for b in range(2):
            for s in range(8):
                send3[c, 8 * b + s] = recv2[c, pl.ds(8 * b + s, 32, stride=16), :]
        start_phase(*phase(2, c))

    ready("c512", "s512", "twist_rows", "sixteen", "sixteen_back")
    c512, s512 = get("c512"), get("s512")
    twist_rows = get("twist_rows")[0]
    sixteen = [r[...] for r in get("sixteen")]
    sixteen_back = [r[...] for r in get("sixteen_back")]
    finish_phase(*phase(2, 0))
    finish_phase(*phase(2, 1))
    x = split(jnp.concatenate([recv3[0], recv3[1]], axis=1))
    lane = lax.broadcasted_iota(jnp.int32, (1, 256), 1)
    sign = jnp.where(lax.rem(lane // 64, 2) == 0, 1.0, -1.0)
    ones_v, twos_v = [], []
    for block in range(4):
        rows = slice(128 * block, 128 * block + 128)
        cosine = mul([r[rows, :] for r in c512], x)
        sine = mul([r[rows, :] for r in s512], x)
        co, si = twist_rows[0, rows, :], twist_rows[1, rows, :]
        one = co * cosine - si * sine
        two = -(si * cosine + co * sine)
        v = split(jnp.concatenate([one, two], axis=1))
        spec = mul(v, sixteen)
        w = wk[rows, :]
        prod_real, prod_imag = spec[:, :128] * w, spec[:, 128:] * w
        send4[0, rows] = prod_real
        send4[1, rows] = prod_imag

        @pl.when(device == 256)
        def _():
            spec2 = mul(split(jnp.concatenate([one * sign, two * sign], axis=1)), sixteen)
            w2 = wk2[rows, :]
            send4[0, rows] = send4[0, rows] + spec2[:, :128] * w2
            send4[1, rows] = send4[1, rows] + spec2[:, 128:] * w2

        prod = split(jnp.concatenate([send4[0, rows], send4[1, rows]], axis=1))
        u = mul(prod, sixteen_back)
        u, ui = u[:, :256], u[:, 256:]
        ones_v.append(u * co + ui * si)
        twos_v.append(ui * co - u * si)
    one = split(jnp.concatenate(ones_v, axis=0))
    two = split(jnp.concatenate(twos_v, axis=0))
    for c in range(2):
        lanes = slice(128 * c, 128 * c + 128)
        one_c, two_c = [v[:, lanes] for v in one], [v[:, lanes] for v in two]
        for block in range(4):
            rows = slice(128 * block, 128 * block + 128)
            send4[c, rows] = mul([r[rows, :] for r in c512], one_c) + mul([r[rows, :] for r in s512], two_c)
        start_phase(*phase(3, c))

    for c in range(2):
        finish_phase(*phase(3, c))
        for g in range(NGX):
            for b in range(2):
                send5[c, 16 * g + 8 * b : 16 * g + 8 * b + 8] = recv4[c, pl.ds(256 * b + g, 8, stride=32), :]
        start_phase(*phase(4, c))

    ready("second_back", "twist_last", "last")
    second_back = [r[...] for r in get("second_back")]
    twist_last = get("twist_last")[0]
    last = [r[...] for r in get("last")]
    for c in range(2):
        finish_phase(*phase(4, c))
        near = [recv5[c, 16 * t : 16 * t + 8] for t in range(32)]
        far = [recv5[c, 16 * (31 - t) + 8 : 16 * (31 - t) + 16] for t in range(32)]
        near, far = jnp.concatenate(near, axis=0), jnp.concatenate(far, axis=0)
        both = jnp.concatenate([near, far], axis=1)
        send6[c] = first_inverse(both[:128], both[128:], second_back, twist_last, last)
        start_phase(*phase(5, c))

    for copy in halos(0):
        copy.wait_recv()
    finish_phase(*phase(5, 0))
    finish_phase(*phase(5, 1))
    for b in range(4):
        padded_pot[8 : 8 + ROWS, 128 * b : 128 * b + 128] = recv6[128 * b : 128 * b + 128, :].T
    edge_rows[2] = padded_pot[8:9, :]
    edge_rows[3] = padded_pot[7 + ROWS : 8 + ROWS, :]
    edge_cols[2] = recv6[0:1, :]
    edge_cols[3] = recv6[COLS - 1 : COLS, :]
    for copy in halos(1):
        copy.start()
    pot_ref[...] = padded_pot[8 : 8 + ROWS, :]
    padded_rho[8 : 8 + ROWS, :] = rho[...]
    padded_rho[7:8, :] = halo_rows[1]
    padded_rho[8 + ROWS : 9 + ROWS, :] = halo_rows[0]
    for copy in halos(1):
        copy.wait_recv()
    padded_pot[7:8, :] = halo_rows[3]
    padded_pot[8 + ROWS : 9 + ROWS, :] = halo_rows[2]
    columns = jnp.concatenate([halo_cols[k] for k in range(4)] + [jnp.zeros((4, ROWS), F32)], axis=0).T
    lane = lax.broadcasted_iota(jnp.int32, (32, COLS), 1)
    for block in range(8):
        base = 8 + 32 * block
        r, p = padded_rho[base : base + 32, :], padded_pot[base : base + 32, :]
        cols = columns[32 * block : 32 * block + 32]
        above = face_flux(r, padded_rho[base + 1 : base + 33, :], p, padded_pot[base + 1 : base + 33, :])
        below = face_flux(padded_rho[base - 1 : base + 31, :], r, padded_pot[base - 1 : base + 31, :], p)
        r_next = jnp.where(lane == COLS - 1, cols[:, 0:1], pltpu.roll(r, COLS - 1, 1))
        p_next = jnp.where(lane == COLS - 1, cols[:, 2:3], pltpu.roll(p, COLS - 1, 1))
        right = face_flux(r, r_next, p, p_next)
        r_edge = jnp.broadcast_to(cols[:, 1:2], (32, 128))
        p_edge = jnp.broadcast_to(cols[:, 3:4], (32, 128))
        first_left = face_flux(r_edge, r[:, :128], p_edge, p[:, :128])[:, 0:1]
        left = jnp.where(lane == 0, first_left, pltpu.roll(right, 1, 1))
        new_ref[32 * block : 32 * block + 32, :] = r - TIME_STEP * ((above - below) + (right - left))

    for p in range(6):
        for c in range(2):
            sent_phase(*phase(p, c))
    for copy in halos(0) + halos(1):
        copy.wait_send()
    weights_copy.wait_send()

    @pl.when(lower)
    def _():
        row_copy.wait_send()


def local(density, kernel_hat):
    constants, index = flat_constants()
    vmem = lambda *shape: pltpu.VMEM(shape, F32)
    n_const = len(constants)
    scratch = [pltpu.VMEM(c.shape, c.dtype) for c in constants] + [
        vmem(ROWS, COLS), vmem(16, N), vmem(8, N), vmem(1, N), vmem(1, N), vmem(512, 128), vmem(512, 128),
        vmem(2, 32, 8, 256), vmem(2, 32, 8, 256),
        vmem(2, 512, 128), vmem(2, 512, 128),
        vmem(2, 16, 32, 128), vmem(2, 512, 128),
        vmem(2, 512, 128), vmem(2, 512, 128),
        vmem(2, 512, 128), vmem(2, 512, 128),
        vmem(2, 256, 256), vmem(512, 256),
        vmem(8, N), vmem(4, 1, COLS), vmem(4, 1, ROWS), vmem(4, 1, COLS), vmem(4, 1, ROWS),
        vmem(ROWS + 16, COLS), vmem(ROWS + 16, COLS),
        pltpu.SemaphoreType.DMA((6, 2, 32)), pltpu.SemaphoreType.DMA((6, 2, 32)),
        pltpu.SemaphoreType.DMA((14,)), pltpu.SemaphoreType.DMA((n_const,)),
        pltpu.SemaphoreType.DMA((2,)), pltpu.SemaphoreType.DMA((2,)),
        pltpu.SemaphoreType.DMA((8,)), pltpu.SemaphoreType.DMA((8,)),
    ]
    out = jax.ShapeDtypeStruct((ROWS, COLS), F32)
    return pl.pallas_call(
        functools.partial(kernel, index, n_const),
        out_shape=(out, out),
        in_specs=[pl.BlockSpec(memory_space=pl.ANY)] * (2 + n_const),
        out_specs=(pl.BlockSpec(memory_space=pltpu.VMEM),) * 2,
        scratch_shapes=scratch,
        compiler_params=pltpu.CompilerParams(
            collective_id=0, has_side_effects=True, vmem_limit_bytes=56 * 1024 * 1024
        ),
        name="convolve_step",
    )(density, kernel_hat, *[jnp.asarray(c) for c in constants])


def solution(mesh):
    return jax.shard_map(
        local, mesh=mesh, in_specs=(P("gx", "gy"), P(("gx", "gy"), None)),
        out_specs=(P("gx", "gy"), P("gx", "gy")), check_vma=False,
    )
```

```python
import functools

import jax
import jax.numpy as jnp
import numpy as np
from jax import lax
from jax.experimental import pallas as pl
from jax.experimental.pallas import tpu as pltpu
from jax.sharding import PartitionSpec as P

TIME_STEP = 0.2
DIFFUSION = 0.25
MESH = pl.DeviceIdType.MESH
F32, BF16 = jnp.float32, jnp.bfloat16
NGX, NGY, N = 32, 16, 8192
ROWS, COLS = 256, 512


def split_np(table):
    table = np.asarray(table, np.float32)
    high = table.astype(BF16)
    low = (table - high.astype(np.float32)).astype(BF16)
    return high, low


def angle(a, b, modulus):
    product = np.asarray(a, np.int64) * np.asarray(b, np.int64) % modulus
    return 2.0 * np.pi * product / modulus


def slot_frequency(half, side, j):
    if half == 0:
        return j + 1 if side == 0 else 16 - j
    return j if side == 0 else 15 - j


@functools.lru_cache(maxsize=None)
def tables():
    t = {}
    eye8 = np.eye(8)
    g = np.arange(32)
    slots = np.arange(16)
    real_rows = np.cos(angle(slots[:, None], g[None], 32))
    imag_rows = -np.sin(angle(slots[:, None], g[None], 32))
    imag_rows[0] = np.cos(angle(16, g, 32))
    t["first"] = split_np(np.kron(np.concatenate([real_rows, imag_rows]), eye8))
    m = np.arange(256)
    theta = angle(slots[:, None], m[None], N)
    last = angle(16, m, N)
    ca, sa, cb, sb = np.cos(theta), np.sin(theta), np.cos(theta), np.sin(theta)
    ca[0], sa[0], cb[0], sb[0] = 0.0, np.cos(last), -np.sin(last), 0.0
    t["twist_first"] = np.repeat(np.stack([ca, sa, cb, sb]), 8, axis=1).astype(np.float32)
    w256 = angle(m[:, None], m[None], 256)
    c256, s256 = np.cos(w256), np.sin(w256)
    forward = np.concatenate([c256, s256], axis=1)
    ones = np.zeros((16, 512))
    ones[0, :256] = 1.0
    t["second"] = split_np(np.concatenate([forward[:128], forward[128:], ones]))
    a = np.arange(512)
    w512 = angle(a[:, None], a[None], 512)
    t["c512"] = split_np(np.cos(w512))
    t["s512"] = split_np(np.sin(w512))
    lane = np.arange(256)
    l16 = 8 * (lane // 128) + lane % 8
    theta = angle(a[:, None], l16[None], N)
    t["twist_rows"] = np.stack([np.cos(theta), np.sin(theta)]).astype(np.float32)
    lin = np.arange(16)
    phi = angle(lin[:, None], lin[None], 16)

    def embed(sign):
        out = np.zeros((2, 2, 8, 8, 2, 16, 8))
        for c in range(2):
            for l8 in range(8):
                co, si = np.cos(phi[8 * c + l8]), sign * np.sin(phi[8 * c + l8])
                for j in range(8):
                    out[c, 0, j, l8, 0, :, j] = co
                    out[c, 0, j, l8, 1, :, j] = si
                    out[c, 1, j, l8, 0, :, j] = -si
                    out[c, 1, j, l8, 1, :, j] = co
        return out.reshape(256, 256)

    def times_i_rows(matrix):
        parts = matrix.reshape(2, 2, 64, -1)
        return np.stack([parts[:, 1], -parts[:, 0]], axis=1).reshape(matrix.shape)

    m2 = embed(-1.0)
    both = np.stack([m2, times_i_rows(m2)]).reshape(2, 2, 128, 256).transpose(1, 0, 2, 3)
    t["sixteen"] = split_np(both.reshape(2, 256, 256))
    inv = np.zeros((2, 16, 8, 2, 2, 8, 8))
    for c in range(2):
        for l8 in range(8):
            co, si = np.cos(phi[8 * c + l8]), np.sin(phi[8 * c + l8])
            for j in range(8):
                inv[0, :, j, c, 0, j, l8] = co
                inv[0, :, j, c, 1, j, l8] = si
                inv[1, :, j, c, 0, j, l8] = -si
                inv[1, :, j, c, 1, j, l8] = co
    turned = np.zeros_like(inv)
    turned[:, :, :, :, 0] = -inv[:, :, :, :, 1]
    turned[:, :, :, :, 1] = inv[:, :, :, :, 0]
    both = np.stack([inv.reshape(256, 2, 128), turned.reshape(256, 2, 128)], axis=2)
    t["sixteen_back"] = split_np(both.transpose(1, 0, 2, 3).reshape(2, 256, 256))
    t["second_back"] = split_np(
        np.concatenate([np.concatenate([c256[:, h], s256[:, h]]) for h in (slice(0, 128), slice(128, 256))])
    )
    freq = np.zeros((2, 2, 2, 8, 8), np.int64)
    for half in range(2):
        for side in range(2):
            for j in range(8):
                freq[half, side, :, j, :] = slot_frequency(half, side, j)
    flat = freq.reshape(2, 256)
    theta = angle(m[None, :, None], flat[:, None, :], N)
    t["twist_last"] = np.stack([np.cos(theta), np.sin(theta)], axis=1).reshape(4, 256, 256).astype(np.float32)
    last = np.zeros((32, 8, 2, 2, 2, 2, 8, 8))
    scale = 2.0 / (float(N) * float(N))
    for half in range(2):
        for side in range(2):
            conj = 1.0 if side == 0 else -1.0
            for j in range(8):
                arc = angle(g, slot_frequency(half, side, j), 32)
                for l in range(8):
                    last[:, l, half, 0, side, 0, j, l] = scale * np.cos(arc)
                    last[:, l, half, 0, side, 1, j, l] = -scale * np.sin(arc) * conj
                    last[:, l, half, 1, side, 0, j, l] = -scale * np.sin(arc)
                    last[:, l, half, 1, side, 1, j, l] = -scale * np.cos(arc) * conj
    t["last"] = split_np(last.reshape(256, 1024))
    flip = np.zeros((512, 512))
    flip[a, (-a) % 512] = 1.0
    t["flip"] = flip.astype(BF16)
    order = np.zeros((2, 16, 8, 16, 8))
    for kb in range(16):
        for s in range(8):
            order[0, kb, s, kb, 7 - s] = 1.0
            order[1, kb, s, kb, (8 - s) % 8] = 1.0
    t["order"] = order.reshape(2, 128, 128).astype(BF16)
    return t


def split(x):
    high = x.astype(BF16)
    return high, (x - high.astype(F32)).astype(BF16)


def mul(a, b, transposed=False):
    dims = (((1,), (1 if transposed else 0,)), ((), ()))
    dot = lambda x, y: lax.dot_general(x, y, dims, preferred_element_type=F32)
    return dot(a[0], b[0]) + (dot(a[0], b[1]) + dot(a[1], b[0]))


def mul_exact(selector, x, transposed=False):
    dims = (((1,), (1 if transposed else 0,)), ((), ()))
    dot = lambda p, q: lax.dot_general(p, q, dims, preferred_element_type=F32)
    high, low = split(x)
    return dot(selector, high) + dot(selector, low)


def first_forward(x, first, twist, second):
    spun = mul(first, split(x))
    real, imag = spun[:128], spun[128:]
    plain = real[:8]
    turned_real = real * twist[0] + imag * twist[1]
    turned_imag = imag * twist[2] - real * twist[3]

    def rows(table, order):
        return [table[8 * s : 8 * s + 8] for s in order]

    outs = []
    for half in range(2):
        if half == 0:
            near, far = list(range(1, 9)), [0] + list(range(15, 8, -1))
            re, im = turned_real, turned_imag
        else:
            near, far = list(range(8)), list(range(15, 7, -1))
            re = jnp.concatenate([plain, turned_real[8:]], axis=0)
            im = jnp.concatenate([jnp.zeros_like(plain), turned_imag[8:]], axis=0)
        cosine = jnp.concatenate(rows(re, near) + rows(im, near) + rows(re, far) + rows(-im, far), axis=0)
        sine = jnp.concatenate(rows(im, near) + rows(-re, near) + rows(im, far) + rows(re, far), axis=0)
        cosine, sine = split(cosine), split(sine)
        picked = slice(0, 128) if half == 0 else slice(128, 272)
        w = [v[picked] for v in second]
        out = mul([v[:, :256] for v in w], cosine, True) + mul([v[:, 256:] for v in w], sine, True)
        outs.append(out)
    low, high = outs[0], outs[1][:128]
    total = outs[1][128:136, :128]
    tile = high[:8, :128]
    row = lax.broadcasted_iota(jnp.int32, (8, 128), 0)
    lane = lax.broadcasted_iota(jnp.int32, (8, 128), 1)
    tile = jnp.where((row == 0) & (lane >= 64) & (lane < 72), pltpu.roll(tile, 64, 1), tile)
    tile = jnp.where((row == 0) & (lane < 8), total, tile)
    near_high = jnp.concatenate([tile, high[8:, :128]], axis=0)
    return low[:, :128], low[:, 128:], near_high, high[:, 128:]


def first_inverse(low, high, second_back, twist, last):
    row = lax.broadcasted_iota(jnp.int32, (8, 128), 0)
    lane = lax.broadcasted_iota(jnp.int32, (8, 128), 1)
    tile = high[:8, :128]
    constant = jnp.where(lane < 8, 0.5 * tile, 0.0)[:1]
    other = jnp.where(lane < 8, 0.5 * pltpu.roll(tile, 64, 1), jnp.where((lane >= 64) & (lane < 72), 0.0, tile))
    tile = jnp.where(row == 0, other, tile)
    top = jnp.concatenate([tile, high[:8, 128:]], axis=1)
    high = jnp.concatenate([top, high[8:]], axis=0)
    total = None
    for half, x in ((0, low), (1, high)):
        spun = mul([v[512 * half : 512 * half + 512] for v in second_back], split(x))
        cosine, sine = spun[:256], spun[256:]
        if half == 1:
            cosine = jnp.concatenate([cosine[:, :128] + constant, cosine[:, 128:]], axis=1)
        co, si = twist[2 * half], twist[2 * half + 1]
        one = co * cosine - si * sine
        two = si * cosine + co * sine
        for k, part in ((0, one), (1, two)):
            at = 512 * half + 256 * k
            term = mul([v[:, at : at + 256] for v in last], split(part), True)
            total = term if total is None else total + term
    return total


def face_flux(lower_rho, upper_rho, lower_pot, upper_pot):
    speed = lower_pot - upper_pot
    drift = jnp.maximum(speed, 0.0) * lower_rho * (1.0 - upper_rho) + jnp.minimum(speed, 0.0) * upper_rho * (
        1.0 - lower_rho
    )
    return drift + DIFFUSION * (lower_rho * lower_rho - upper_rho * upper_rho)


def direct_layout(own):
    return 0.5 * jnp.concatenate([own[:, 512 * b : 512 * b + 512] for b in range(16)], axis=0).T


def mirror_layout(other, flip, order):
    mirror = jnp.concatenate([other[:, 512 * (15 - b) : 512 * (15 - b) + 512] for b in range(16)], axis=0)
    turned = mul_exact(flip, mirror, True)
    top = turned[:8]
    row = lax.broadcasted_iota(jnp.int32, (8, 128), 0)
    top = jnp.where(row == 0, pltpu.roll(top, 8, 1), top)
    turned = jnp.concatenate([top, turned[8:]], axis=0)
    high, low = split(turned)
    dot = lambda x: jnp.dot(x, order, preferred_element_type=F32)
    return 0.5 * (dot(high) + dot(low))


CONSTANTS = (
    "first", "twist_first", "second", "c512", "s512", "twist_rows", "sixteen", "sixteen_back",
    "second_back", "twist_last", "last", "flip", "order",
)


def flat_constants():
    out, index = [], {}
    for name in CONSTANTS:
        value = tables()[name]
        value = value if isinstance(value, tuple) else (value,)
        index[name] = list(range(len(out), len(out) + len(value)))
        out.extend(value)
    return out, index


def kernel(index, n_const, *refs):
    rho_ref, kernel_ref = refs[:2]
    const_hbm = refs[2 : 2 + n_const]
    pot_ref, div_ref = refs[2 + n_const : 4 + n_const]
    rest = list(refs[4 + n_const :])
    const = [rest.pop(0) for _ in range(n_const)]
    (
        rho, weights, weights_mid, weights_turned, weights_got, row0_send, row0_mid, row0_got, only, wk, wk2, spec, spec2,
        send1, recv1, send2, recv2, send3, recv3, send4, recv4, send5, recv5, send6, recv6,
        edge_rows, edge_cols, halo_rows, halo_cols, padded_rho, padded_pot, pot_out, div_out,
        send_sem, recv_sem, local_sem, load_sem, const_sem, k_send, k_recv, halo_send, halo_recv,
    ) = rest
    gx, gy = lax.axis_index("gx"), lax.axis_index("gy")
    x_low, y_at, core = gx // 16, lax.rem(gx // 2, 8), lax.rem(gx, 2)
    z_at, x_high = gy // 2, lax.rem(gy, 2)
    device = gx * NGY + gy
    lower = gx < NGX // 2

    def get(name):
        return [const[i] for i in index[name]]

    barrier = pltpu.get_barrier_semaphore()

    def greet(axis, n, me):
        def body(i, carry):
            pl.semaphore_signal(barrier, inc=1, device_id={axis: lax.rem(me + i, n)}, device_id_type=MESH)
            return carry

        lax.fori_loop(1, n, body, 0)

    greet("gx", NGX, gx)
    greet("gy", NGY, gy)

    load_rho = pltpu.make_async_copy(rho_ref, rho, load_sem.at[0])
    load_weights = pltpu.make_async_copy(kernel_ref, weights, load_sem.at[1])
    load_rho.start()
    load_weights.start()
    loads = [pltpu.make_async_copy(const_hbm[i], const[i], const_sem.at[i]) for i in range(n_const)]
    for load in loads:
        load.start()

    def ready(*names):
        for name in names:
            for i in index[name]:
                loads[i].wait()

    load_rho.wait()
    for b in range(4):
        turned = rho[:, 128 * b : 128 * b + 128].T
        for part in range(8):
            for c in range(2):
                send1[c, 8 * b + part] = turned[16 * part + 8 * c : 16 * part + 8 * c + 8]
    edge_rows[0] = rho[0:1, :]
    edge_rows[1] = rho[ROWS - 1 : ROWS, :]
    edge_cols[0] = send1[0, 0, 0:1, :]
    edge_cols[1] = send1[1, NGX - 1, 7:8, :]
    load_weights.wait()
    row0_send[...] = weights[0:1, :]

    @pl.when(lax.rem(gy, 8) == 0)
    def _():
        row0_mid[...] = weights[0:1, :]

    pl.semaphore_wait(barrier, NGX - 1 + NGY - 1)

    def far_first(t):
        return jnp.where(lax.rem(t, 2) == 1, 4 - (t + 1) // 2, 4 + t // 2)

    def peer_gx(i):
        x = lax.rem(x_low + 1 - i // 16, 2)
        y = lax.rem(y_at + far_first(lax.rem(i, 16) // 2), 8)
        return x * 16 + y * 2 + lax.rem(core + 1 - lax.rem(i, 2), 2)

    def peer_gy(i):
        return lax.rem(z_at + far_first(i // 2), 8) * 2 + lax.rem(x_high + 1 - lax.rem(i, 2), 2)

    def slot_of(y):
        q, b = y // 2, lax.rem(y, 2)
        return b * 8 + jnp.where(b == 0, q, 7 - q)

    def at(ref, where, start, size):
        return ref.at[(*where, pl.ds(pl.multiple_of(start, 8), size))]

    def ends(p, c, h, to):
        half = 16 * lax.rem(x_low + 1 - h, 2)
        if p == 0:
            return send1.at[c, to], recv1.at[c, gx]
        if p == 1:
            return at(send2, (c,), to * 16, 16), at(recv2, (c,), 256 * h + lax.rem(gx, 16) * 16, 16)
        if p == 2:
            return at(send3, (c,), 256 * h + slot_of(to) * 16, 16), at(recv3, (c,), gy * 32 + half, 16)
        if p == 3:
            return at(send4, (c,), to * 32 + half, 16), at(recv4, (c,), 256 * h + slot_of(gy) * 16, 16)
        if p == 4:
            return at(send5, (c,), 256 * h + lax.rem(to, 16) * 16, 16), at(recv5, (c,), gx * 16, 16)
        return at(send6, (c,), to * 8, 8), recv6.at[pl.ds(pl.multiple_of(gx * 16 + 8 * c, 8), 8)]

    def message(p, c, h, i):
        over_gy = p in (2, 3)
        to = peer_gy(i) if over_gy else peer_gx(i + 16 * h)
        source, target = ends(p, c, h, to)
        return pltpu.make_async_remote_copy(
            src_ref=source, dst_ref=target, send_sem=send_sem.at[p, c], recv_sem=recv_sem.at[p, c, h],
            device_id={"gy" if over_gy else "gx": to}, device_id_type=MESH,
        )

    def count(p, h):
        return 16 if p not in (2, 3) and h == 0 else 15

    def own_copy(p, c, h):
        source, target = ends(p, c, h, gy if p in (2, 3) else gx)
        return pltpu.make_async_copy(source, target, local_sem.at[p, c, h])

    def start(p, c, h):
        def body(i, carry):
            message(p, c, h, i).start()
            return carry

        if count(p, h) == 15:
            own_copy(p, c, h).start()
        lax.fori_loop(0, count(p, h), body, 0)

    def group(some, p, c, h):
        return pltpu.make_async_remote_copy(
            src_ref=some, dst_ref=some, send_sem=send_sem.at[p, c], recv_sem=recv_sem.at[p, c, h],
            device_id={"gx": lax.rem(gx + 1, NGX)}, device_id_type=MESH,
        )

    def finish(p, c, h):
        n = count(p, h)
        if n == 15:
            own_copy(p, c, h).wait()
        if p == 0:
            some = recv1.at[c, pl.ds(0, n)]
        elif p == 5:
            some = recv6.at[pl.ds(0, 8 * n)]
        else:
            some = (None, recv2, recv3, recv4, recv5)[p].at[c, pl.ds(0, 16 * n)]
        group(some, p, c, h).wait_recv()

    def sent(p, c):
        if p == 0:
            some = send1.at[c, pl.ds(0, 31)]
        elif p == 5:
            some = send6.at[c, pl.ds(0, 8 * 31)]
        else:
            some = (None, send2, send3, send4, send5)[p].at[c, pl.ds(0, 16 * (30 if p in (2, 3) else 31))]
        group(some, p, c, 0).wait_send()

    def halo(which, kind, k):
        axis, n, me = (("gx", NGX, gx), ("gy", NGY, gy))[kind]
        to = lax.rem(me + (n - 1 if k == 0 else 1), n)
        source, target = ((edge_rows, halo_rows), (edge_cols, halo_cols))[kind]
        return pltpu.make_async_remote_copy(
            src_ref=source.at[2 * which + k], dst_ref=target.at[2 * which + k],
            send_sem=halo_send.at[4 * which + 2 * kind + k], recv_sem=halo_recv.at[4 * which + 2 * kind + k],
            device_id={axis: to}, device_id_type=MESH,
        )

    def relay(source, target, k, where):
        return pltpu.make_async_remote_copy(
            src_ref=source, dst_ref=target, send_sem=k_send.at[k], recv_sem=k_recv.at[k], device_id=where,
            device_id_type=MESH,
        )

    weights_first = relay(weights.at[pl.ds(8, 8)], weights_mid, 0, {"gy": NGY - 1 - gy})
    weights_second = relay(weights_turned, weights_got, 1, {"gx": NGX - 1 - gx})
    row_first = relay(row0_send, row0_mid, 2, {"gy": lax.rem(NGY - gy, NGY)})
    edge_gx = jnp.where(gx == 0, 16, jnp.where(gx == 16, 0, lax.rem(NGX - gx, NGX)))
    row_second = relay(row0_mid, row0_got, 3, {"gx": jnp.where(gy == 0, edge_gx, NGX - 1 - gx)})
    row_moves = lower & (lax.rem(gy, 8) != 0)

    for c in range(2):
        for h in range(2):
            start(0, c, h)
    weights_first.start()

    @pl.when(row_moves)
    def _():
        row_first.start()

    for kind in range(2):
        for k in range(2):
            halo(0, kind, k).start()

    wk[...] = direct_layout(jnp.where(lower, weights[1:9, :], weights[0:8, :]))

    @pl.when(row_moves)
    def _():
        row_first.wait_recv()

    @pl.when(lower)
    def _():
        row_second.start()

    ready("first", "twist_first", "second")
    first, second, twist_first = get("first"), get("second"), get("twist_first")[0]
    for c in range(2):
        finish(0, c, 0)
        finish(0, c, 1)
        x = recv1[c].reshape(256, 256)
        near_low, far_low, near_high, far_high = first_forward(
            x, [r[...] for r in first], twist_first, [r[...] for r in second]
        )
        for t in range(16):
            rows = slice(8 * t, 8 * t + 8)
            send2[c, 16 * t : 16 * t + 8] = near_low[rows]
            send2[c, 16 * (16 + t) : 16 * (16 + t) + 8] = near_high[rows]
            send2[c, 16 * (31 - t) + 8 : 16 * (31 - t) + 16] = far_low[rows]
            send2[c, 16 * (15 - t) + 8 : 16 * (15 - t) + 16] = far_high[rows]
        start(1, c, 0)
        start(1, c, 1)

    ready("flip", "order")
    flip = get("flip")[0][...]
    order_ref = get("order")[0]
    weights_first.wait_recv()

    @pl.when(lower)
    def _():
        weights_mid[0:1, :] = jnp.zeros((1, N), F32)
        weights_turned[...] = mirror_layout(weights_mid[...], flip, order_ref[1])

    @pl.when(jnp.logical_not(lower))
    def _():
        weights_turned[...] = mirror_layout(weights_mid[...], flip, order_ref[0])

    weights_second.start()

    @pl.when(jnp.logical_not(lower))
    def _():
        row_second.wait_recv()
        row = lax.broadcasted_iota(jnp.int32, (8, N), 0)

        @pl.when(device == 256)
        def _():
            one, two = weights[0:1, :], row0_got[...]
            only[...] = jnp.where(row == 0, jnp.broadcast_to(0.5 * (two - one), (8, N)), 0.0)
            change = direct_layout(only[...])
            wk[...] = wk[...] + change
            wk2[...] = change + mirror_layout(only[...], flip, order_ref[1])
            row0_got[...] = 0.5 * (one + two)

        only[...] = jnp.where(row == 0, jnp.broadcast_to(row0_got[...], (8, N)), 0.0)
        wk[...] = wk[...] + mirror_layout(only[...], flip, order_ref[1])

    for c in range(2):
        for h in range(2):
            finish(1, c, h)
            for slot in range(16):
                rows = slice(256 * h + 16 * slot, 256 * h + 16 * slot + 16)
                send3[c, rows] = recv2[c, pl.ds(256 * h + slot, 16, stride=16), :]
            start(2, c, h)

    ready("c512", "s512", "twist_rows", "sixteen", "sixteen_back")
    c512, s512 = [r[...] for r in get("c512")], [r[...] for r in get("s512")]
    twist_rows, sixteen, sixteen_back = get("twist_rows")[0], get("sixteen"), get("sixteen_back")
    lane = lax.broadcasted_iota(jnp.int32, (1, 128), 1)
    sign = jnp.where(lane < 64, 1.0, -1.0)
    for c in range(2):
        lanes = slice(128 * c, 128 * c + 128)
        finish(2, c, 0)
        finish(2, c, 1)
        x = split(recv3[c])
        cosine, sine = mul(c512, x), mul(s512, x)
        co, si = twist_rows[0, :, lanes], twist_rows[1, :, lanes]
        one = co * cosine - si * sine
        two = -(si * cosine + co * sine)
        matrix = [r[c] for r in sixteen]
        part = mul(split(jnp.concatenate([one, two], axis=1)), matrix)
        spec[...] = part if c == 0 else spec[...] + part

        @pl.when(device == 256)
        def _():
            part = mul(split(jnp.concatenate([one * sign, two * sign], axis=1)), matrix)
            spec2[...] = part if c == 0 else spec2[...] + part

    weights_second.wait_recv()
    both_weights = wk[...] + weights_got[...]
    spec[:, :128] = spec[:, :128] * both_weights
    spec[:, 128:] = spec[:, 128:] * both_weights

    @pl.when(device == 256)
    def _():
        spec[:, :128] = spec[:, :128] + spec2[:, :128] * wk2[...]
        spec[:, 128:] = spec[:, 128:] + spec2[:, 128:] * wk2[...]

    prod = split(spec[...])
    for c in range(2):
        lanes = slice(128 * c, 128 * c + 128)
        u = mul(prod, [r[c] for r in sixteen_back])
        u, ui = u[:, :128], u[:, 128:]
        co, si = twist_rows[0, :, lanes], twist_rows[1, :, lanes]
        send4[c] = mul(c512, split(u * co + ui * si)) + mul(s512, split(ui * co - u * si))
        start(3, c, 0)
        start(3, c, 1)

    for c in range(2):
        for h in range(2):
            finish(3, c, h)
            for r in range(16):
                for b in range(2):
                    base = 256 * h + 16 * r + 8 * b
                    send5[c, base : base + 8] = recv4[c, pl.ds(256 * h + 128 * b + r, 8, stride=16), :]
            start(4, c, h)

    ready("second_back", "twist_last", "last")
    second_back = [r[...] for r in get("second_back")]
    twist_last = get("twist_last")[0]
    last = [r[...] for r in get("last")]
    for c in range(2):
        finish(4, c, 0)
        finish(4, c, 1)
        near = [recv5[c, 16 * t : 16 * t + 8] for t in range(32)]
        far = [recv5[c, 16 * (31 - t) + 8 : 16 * (31 - t) + 16] for t in range(32)]
        near, far = jnp.concatenate(near, axis=0), jnp.concatenate(far, axis=0)
        both = jnp.concatenate([near, far], axis=1)
        send6[c] = first_inverse(both[:128], both[128:], second_back, twist_last, last)
        start(5, c, 0)
        start(5, c, 1)

    padded_rho[8 : 8 + ROWS, :] = rho[...]
    for kind in range(2):
        for k in range(2):
            halo(0, kind, k).wait_recv()
    padded_rho[7:8, :] = halo_rows[1]
    padded_rho[8 + ROWS : 9 + ROWS, :] = halo_rows[0]
    for c in range(2):
        for h in range(2):
            finish(5, c, h)
    edge_cols[2] = recv6[0:1, :]
    edge_cols[3] = recv6[COLS - 1 : COLS, :]
    for k in range(2):
        halo(1, 1, k).start()
    for b in range(4):
        padded_pot[8 : 8 + ROWS, 128 * b : 128 * b + 128] = recv6[128 * b : 128 * b + 128, :].T
    edge_rows[2] = padded_pot[8:9, :]
    edge_rows[3] = padded_pot[7 + ROWS : 8 + ROWS, :]
    for k in range(2):
        halo(1, 0, k).start()
    pot_out[...] = 0.5 * padded_pot[8 : 8 + ROWS, :]
    pot_store = pltpu.make_async_copy(pot_out, pot_ref, load_sem.at[2])
    pot_store.start()
    for k in range(2):
        halo(1, 1, k).wait_recv()
    columns = jnp.concatenate([halo_cols[k] for k in range(4)] + [jnp.zeros((4, ROWS), F32)], axis=0).T
    lane = lax.broadcasted_iota(jnp.int32, (32, COLS), 1)
    for block in (1, 2, 3, 4, 5, 6, 0, 7):
        if block == 0:
            for k in range(2):
                halo(1, 0, k).wait_recv()
            padded_pot[7:8, :] = halo_rows[3]
            padded_pot[8 + ROWS : 9 + ROWS, :] = halo_rows[2]
        base = 8 + 32 * block
        r, p = padded_rho[base : base + 32, :], padded_pot[base : base + 32, :]
        cols = columns[32 * block : 32 * block + 32]
        above = face_flux(r, padded_rho[base + 1 : base + 33, :], p, padded_pot[base + 1 : base + 33, :])
        below = face_flux(padded_rho[base - 1 : base + 31, :], r, padded_pot[base - 1 : base + 31, :], p)
        r_next = jnp.where(lane == COLS - 1, cols[:, 0:1], pltpu.roll(r, COLS - 1, 1))
        p_next = jnp.where(lane == COLS - 1, cols[:, 2:3], pltpu.roll(p, COLS - 1, 1))
        right = face_flux(r, r_next, p, p_next)
        r_edge = jnp.broadcast_to(cols[:, 1:2], (32, 128))
        p_edge = jnp.broadcast_to(cols[:, 3:4], (32, 128))
        first_left = face_flux(r_edge, r[:, :128], p_edge, p[:, :128])[:, 0:1]
        left = jnp.where(lane == 0, first_left, pltpu.roll(right, 1, 1))
        div_out[32 * block : 32 * block + 32, :] = (above - below) + (right - left)
    div_store = pltpu.make_async_copy(div_out, div_ref, load_sem.at[3])
    div_store.start()

    for p in range(6):
        for c in range(2):
            sent(p, c)
    for which in range(2):
        for kind in range(2):
            for k in range(2):
                halo(which, kind, k).wait_send()
    weights_first.wait_send()
    weights_second.wait_send()

    @pl.when(row_moves)
    def _():
        row_first.wait_send()

    @pl.when(lower)
    def _():
        row_second.wait_send()

    pot_store.wait()
    div_store.wait()


def local(density, kernel_hat):
    constants, index = flat_constants()
    vmem = lambda *shape: pltpu.VMEM(shape, F32)
    dma = lambda *shape: pltpu.SemaphoreType.DMA(shape)
    n_const = len(constants)
    scratch = [pltpu.VMEM(c.shape, c.dtype) for c in constants] + [
        vmem(ROWS, COLS), vmem(16, N), vmem(8, N), vmem(512, 128), vmem(512, 128), vmem(1, N), vmem(1, N), vmem(1, N), vmem(8, N),
        vmem(512, 128), vmem(512, 128), vmem(512, 256), vmem(512, 256),
        vmem(2, 32, 8, 256), vmem(2, 32, 8, 256),
        vmem(2, 512, 128), vmem(2, 512, 128), vmem(2, 512, 128), vmem(2, 512, 128),
        vmem(2, 512, 128), vmem(2, 512, 128), vmem(2, 512, 128), vmem(2, 512, 128),
        vmem(2, 256, 256), vmem(512, 256),
        vmem(4, 1, COLS), vmem(4, 1, ROWS), vmem(4, 1, COLS), vmem(4, 1, ROWS),
        vmem(ROWS + 16, COLS), vmem(ROWS + 16, COLS), vmem(ROWS, COLS), vmem(ROWS, COLS),
        dma(6, 2), dma(6, 2, 2), dma(6, 2, 2), dma(4), dma(n_const), dma(4), dma(4), dma(8), dma(8),
    ]
    out = jax.ShapeDtypeStruct((ROWS, COLS), F32)
    half_potential, divergence = pl.pallas_call(
        functools.partial(kernel, index, n_const),
        out_shape=(out, out),
        in_specs=[pl.BlockSpec(memory_space=pl.ANY)] * (2 + n_const),
        out_specs=(pl.BlockSpec(memory_space=pl.ANY),) * 2,
        scratch_shapes=scratch,
        compiler_params=pltpu.CompilerParams(
            collective_id=0, has_side_effects=True, vmem_limit_bytes=56 * 1024 * 1024
        ),
        name="convolve_step",
    )(density, kernel_hat, *[jnp.asarray(c) for c in constants])
    return 2.0 * half_potential, density - TIME_STEP * divergence


def solution(mesh):
    return jax.shard_map(
        local, mesh=mesh, in_specs=(P("gx", "gy"), P(("gx", "gy"), None)),
        out_specs=(P("gx", "gy"), P("gx", "gy")), check_vma=False,
    )
```

```python
import functools

import jax
import jax.numpy as jnp
import numpy as np
from jax import lax
from jax.experimental import pallas as pl
from jax.experimental.pallas import tpu as pltpu
from jax.sharding import PartitionSpec as P

TIME_STEP = 0.2
DIFFUSION = 0.25
MESH = pl.DeviceIdType.MESH
F32, BF16 = jnp.float32, jnp.bfloat16
NGX, NGY, N = 32, 16, 8192
ROWS, COLS = 256, 512


def split_np(table):
    table = np.asarray(table, np.float32)
    high = table.astype(BF16)
    low = (table - high.astype(np.float32)).astype(BF16)
    return high, low


def angle(a, b, modulus):
    product = np.asarray(a, np.int64) * np.asarray(b, np.int64) % modulus
    return 2.0 * np.pi * product / modulus


def slot_frequency(half, side, j):
    if half == 0:
        return j + 1 if side == 0 else 16 - j
    return j if side == 0 else 15 - j


@functools.lru_cache(maxsize=None)
def tables():
    t = {}
    eye8 = np.eye(8)
    g = np.arange(32)
    slots = np.arange(16)
    real_rows = np.cos(angle(slots[:, None], g[None], 32))
    imag_rows = -np.sin(angle(slots[:, None], g[None], 32))
    imag_rows[0] = np.cos(angle(16, g, 32))
    t["first"] = split_np(np.kron(np.concatenate([real_rows, imag_rows]), eye8))
    m = np.arange(256)
    theta = angle(slots[:, None], m[None], N)
    last = angle(16, m, N)
    ca, sa, cb, sb = np.cos(theta), np.sin(theta), np.cos(theta), np.sin(theta)
    ca[0], sa[0], cb[0], sb[0] = 0.0, np.cos(last), -np.sin(last), 0.0
    t["twist_first"] = np.repeat(np.stack([ca, sa, cb, sb]), 8, axis=1).astype(np.float32)
    w256 = angle(m[:, None], m[None], 256)
    c256, s256 = np.cos(w256), np.sin(w256)
    forward = np.concatenate([c256, s256], axis=1)
    ones = np.zeros((16, 512))
    ones[0, :256] = 1.0
    t["second"] = split_np(np.concatenate([forward[:128], forward[128:], ones]))
    a = np.arange(512)
    w512 = angle(a[:, None], a[None], 512)
    t["c512"] = split_np(np.cos(w512))
    t["s512"] = split_np(np.sin(w512))
    lane = np.arange(256)
    l16 = 8 * (lane // 128) + lane % 8
    theta = angle(a[:, None], l16[None], N)
    t["twist_rows"] = np.stack([np.cos(theta), np.sin(theta)]).astype(np.float32)
    lin = np.arange(16)
    phi = angle(lin[:, None], lin[None], 16)

    def embed(sign):
        out = np.zeros((2, 2, 8, 8, 2, 16, 8))
        for c in range(2):
            for l8 in range(8):
                co, si = np.cos(phi[8 * c + l8]), sign * np.sin(phi[8 * c + l8])
                for j in range(8):
                    out[c, 0, j, l8, 0, :, j] = co
                    out[c, 0, j, l8, 1, :, j] = si
                    out[c, 1, j, l8, 0, :, j] = -si
                    out[c, 1, j, l8, 1, :, j] = co
        return out.reshape(256, 256)

    def times_i_rows(matrix):
        parts = matrix.reshape(2, 2, 64, -1)
        return np.stack([parts[:, 1], -parts[:, 0]], axis=1).reshape(matrix.shape)

    m2 = embed(-1.0)
    both = np.stack([m2, times_i_rows(m2)]).reshape(2, 2, 128, 256).transpose(1, 0, 2, 3)
    t["sixteen"] = split_np(both.reshape(2, 256, 256))
    inv = np.zeros((2, 16, 8, 2, 2, 8, 8))
    for c in range(2):
        for l8 in range(8):
            co, si = np.cos(phi[8 * c + l8]), np.sin(phi[8 * c + l8])
            for j in range(8):
                inv[0, :, j, c, 0, j, l8] = co
                inv[0, :, j, c, 1, j, l8] = si
                inv[1, :, j, c, 0, j, l8] = -si
                inv[1, :, j, c, 1, j, l8] = co
    turned = np.zeros_like(inv)
    turned[:, :, :, :, 0] = -inv[:, :, :, :, 1]
    turned[:, :, :, :, 1] = inv[:, :, :, :, 0]
    both = np.stack([inv.reshape(256, 2, 128), turned.reshape(256, 2, 128)], axis=2)
    t["sixteen_back"] = split_np(both.transpose(1, 0, 2, 3).reshape(2, 256, 256))
    t["second_back"] = split_np(
        np.concatenate([np.concatenate([c256[:, h], s256[:, h]]) for h in (slice(0, 128), slice(128, 256))])
    )
    freq = np.zeros((2, 2, 2, 8, 8), np.int64)
    for half in range(2):
        for side in range(2):
            for j in range(8):
                freq[half, side, :, j, :] = slot_frequency(half, side, j)
    flat = freq.reshape(2, 256)
    theta = angle(m[None, :, None], flat[:, None, :], N)
    t["twist_last"] = np.stack([np.cos(theta), np.sin(theta)], axis=1).reshape(4, 256, 256).astype(np.float32)
    last = np.zeros((32, 8, 2, 2, 2, 2, 8, 8))
    scale = 2.0 / (float(N) * float(N))
    for half in range(2):
        for side in range(2):
            conj = 1.0 if side == 0 else -1.0
            for j in range(8):
                arc = angle(g, slot_frequency(half, side, j), 32)
                for l in range(8):
                    last[:, l, half, 0, side, 0, j, l] = scale * np.cos(arc)
                    last[:, l, half, 0, side, 1, j, l] = -scale * np.sin(arc) * conj
                    last[:, l, half, 1, side, 0, j, l] = -scale * np.sin(arc)
                    last[:, l, half, 1, side, 1, j, l] = -scale * np.cos(arc) * conj
    t["last"] = split_np(last.reshape(256, 1024))
    flip = np.zeros((512, 512))
    flip[a, (-a) % 512] = 1.0
    t["flip"] = flip.astype(BF16)
    order = np.zeros((2, 16, 8, 16, 8))
    for kb in range(16):
        for s in range(8):
            order[0, kb, s, kb, 7 - s] = 1.0
            order[1, kb, s, kb, (8 - s) % 8] = 1.0
    t["order"] = order.reshape(2, 128, 128).astype(BF16)
    return t


def split(x):
    high = x.astype(BF16)
    return high, (x - high.astype(F32)).astype(BF16)


def mul(a, b, transposed=False):
    dims = (((1,), (1 if transposed else 0,)), ((), ()))
    dot = lambda x, y: lax.dot_general(x, y, dims, preferred_element_type=F32)
    return dot(a[0], b[0]) + (dot(a[0], b[1]) + dot(a[1], b[0]))


def mul_exact(selector, x, transposed=False):
    dims = (((1,), (1 if transposed else 0,)), ((), ()))
    dot = lambda p, q: lax.dot_general(p, q, dims, preferred_element_type=F32)
    high, low = split(x)
    return dot(selector, high) + dot(selector, low)


def first_forward(x, first, twist, second):
    spun = mul(first, split(x))
    real, imag = spun[:128], spun[128:]
    plain = real[:8]
    turned_real = real * twist[0] + imag * twist[1]
    turned_imag = imag * twist[2] - real * twist[3]

    def rows(table, order):
        return [table[8 * s : 8 * s + 8] for s in order]

    outs = []
    for half in range(2):
        if half == 0:
            near, far = list(range(1, 9)), [0] + list(range(15, 8, -1))
            re, im = turned_real, turned_imag
        else:
            near, far = list(range(8)), list(range(15, 7, -1))
            re = jnp.concatenate([plain, turned_real[8:]], axis=0)
            im = jnp.concatenate([jnp.zeros_like(plain), turned_imag[8:]], axis=0)
        cosine = jnp.concatenate(rows(re, near) + rows(im, near) + rows(re, far) + rows(-im, far), axis=0)
        sine = jnp.concatenate(rows(im, near) + rows(-re, near) + rows(im, far) + rows(re, far), axis=0)
        cosine, sine = split(cosine), split(sine)
        picked = slice(0, 128) if half == 0 else slice(128, 272)
        w = [v[picked] for v in second]
        out = mul([v[:, :256] for v in w], cosine, True) + mul([v[:, 256:] for v in w], sine, True)
        outs.append(out)
    low, high = outs[0], outs[1][:128]
    total = outs[1][128:136, :128]
    tile = high[:8, :128]
    row = lax.broadcasted_iota(jnp.int32, (8, 128), 0)
    lane = lax.broadcasted_iota(jnp.int32, (8, 128), 1)
    tile = jnp.where((row == 0) & (lane >= 64) & (lane < 72), pltpu.roll(tile, 64, 1), tile)
    tile = jnp.where((row == 0) & (lane < 8), total, tile)
    near_high = jnp.concatenate([tile, high[8:, :128]], axis=0)
    return low[:, :128], low[:, 128:], near_high, high[:, 128:]


def first_inverse(low, high, second_back, twist, last):
    row = lax.broadcasted_iota(jnp.int32, (8, 128), 0)
    lane = lax.broadcasted_iota(jnp.int32, (8, 128), 1)
    tile = high[:8, :128]
    constant = jnp.where(lane < 8, 0.5 * tile, 0.0)[:1]
    other = jnp.where(lane < 8, 0.5 * pltpu.roll(tile, 64, 1), jnp.where((lane >= 64) & (lane < 72), 0.0, tile))
    tile = jnp.where(row == 0, other, tile)
    top = jnp.concatenate([tile, high[:8, 128:]], axis=1)
    high = jnp.concatenate([top, high[8:]], axis=0)
    total = None
    for half, x in ((0, low), (1, high)):
        spun = mul([v[512 * half : 512 * half + 512] for v in second_back], split(x))
        cosine, sine = spun[:256], spun[256:]
        if half == 1:
            cosine = jnp.concatenate([cosine[:, :128] + constant, cosine[:, 128:]], axis=1)
        co, si = twist[2 * half], twist[2 * half + 1]
        one = co * cosine - si * sine
        two = si * cosine + co * sine
        for k, part in ((0, one), (1, two)):
            at = 512 * half + 256 * k
            term = mul([v[:, at : at + 256] for v in last], split(part), True)
            total = term if total is None else total + term
    return total


def face_flux(lower_rho, upper_rho, lower_pot, upper_pot):
    speed = lower_pot - upper_pot
    drift = jnp.maximum(speed, 0.0) * lower_rho * (1.0 - upper_rho) + jnp.minimum(speed, 0.0) * upper_rho * (
        1.0 - lower_rho
    )
    return drift + DIFFUSION * (lower_rho * lower_rho - upper_rho * upper_rho)


def direct_layout(own):
    return 0.5 * jnp.concatenate([own[:, 512 * b : 512 * b + 512] for b in range(16)], axis=0).T


def mirror_layout(other, flip, order):
    mirror = jnp.concatenate([other[:, 512 * (15 - b) : 512 * (15 - b) + 512] for b in range(16)], axis=0)
    turned = mul_exact(flip, mirror, True)
    top = turned[:8]
    row = lax.broadcasted_iota(jnp.int32, (8, 128), 0)
    top = jnp.where(row == 0, pltpu.roll(top, 8, 1), top)
    turned = jnp.concatenate([top, turned[8:]], axis=0)
    high, low = split(turned)
    dot = lambda x: jnp.dot(x, order, preferred_element_type=F32)
    return 0.5 * (dot(high) + dot(low))


CONSTANTS = (
    "first", "twist_first", "second", "c512", "s512", "twist_rows", "sixteen", "sixteen_back",
    "second_back", "twist_last", "last", "flip", "order",
)


def flat_constants():
    out, index = [], {}
    for name in CONSTANTS:
        value = tables()[name]
        value = value if isinstance(value, tuple) else (value,)
        index[name] = list(range(len(out), len(out) + len(value)))
        out.extend(value)
    return out, index


def pack(values):
    pieces, stacks = [], ([], [])
    for i, value in enumerate(values):
        which = 0 if value.dtype == np.float32 else 1
        planes = value if value.ndim == 3 else value[None]
        for k, plane in enumerate(planes):
            begin = sum(p.shape[0] for p in stacks[which])
            pieces.append((i, k if value.ndim == 3 else None, which, begin, *plane.shape))
            stacks[which].append(np.pad(plane, ((0, 0), (0, 1024 - plane.shape[1]))))
    return pieces, [np.concatenate(stack) for stack in stacks]


def kernel(index, n_const, pieces, *refs):
    rho_ref, kernel_ref = refs[:2]
    packs = refs[2:4]
    pot_ref, new_ref = refs[4:6]
    rest = list(refs[6:])
    const = [rest.pop(0) for _ in range(n_const)]
    (
        rho, weights, weights_mid, weights_turned, weights_got, row0_send, row0_mid, row0_got, only, wk, wk2, spec, spec2,
        send1, recv1, send2, recv2, send3, recv3, send4, recv4, send5, recv5, send6, recv6,
        edge_rows, edge_cols, halo_rows, halo_cols, padded_rho, padded_pot, pot_out, new_out,
        send_sem, recv_sem, local_sem, load_sem, const_sem, k_send, k_recv, halo_send, halo_recv,
    ) = rest
    gx, gy = lax.axis_index("gx"), lax.axis_index("gy")
    x_low, y_at, core = gx // 16, lax.rem(gx // 2, 8), lax.rem(gx, 2)
    z_at, x_high = gy // 2, lax.rem(gy, 2)
    device = gx * NGY + gy
    lower = gx < NGX // 2

    def get(name):
        return [const[i] for i in index[name]]

    barrier = pltpu.get_barrier_semaphore()

    def greet(axis, n, me):
        def body(i, carry):
            pl.semaphore_signal(barrier, inc=1, device_id={axis: lax.rem(me + i, n)}, device_id_type=MESH)
            return carry

        lax.fori_loop(1, n, body, 0)

    across = {"gx": gx + 16 - 32 * x_low, "gy": NGY - 1 - gy}
    pl.semaphore_signal(barrier, inc=1, device_id=across, device_id_type=MESH)
    greet("gx", NGX, gx)
    greet("gy", NGY, gy)

    load_rho = pltpu.make_async_copy(rho_ref, rho, load_sem.at[0])
    load_weights = pltpu.make_async_copy(kernel_ref, weights, load_sem.at[1])
    load_rho.start()
    load_weights.start()
    loads = [[] for _ in range(n_const)]
    for at_piece, (i, k, which, begin, rows, width) in enumerate(pieces):
        source = packs[which].at[pl.ds(begin, rows), pl.ds(0, width)]
        target = const[i] if k is None else const[i].at[k]
        load = pltpu.make_async_copy(source, target, const_sem.at[at_piece])
        load.start()
        loads[i].append(load)

    def ready(*names):
        for name in names:
            for i in index[name]:
                for load in loads[i]:
                    load.wait()

    load_rho.wait()
    for b in range(4):
        turned = rho[:, 128 * b : 128 * b + 128].T
        for part in range(8):
            for c in range(2):
                send1[c, 8 * b + part] = turned[16 * part + 8 * c : 16 * part + 8 * c + 8]
    edge_rows[0] = rho[0:1, :]
    edge_rows[1] = rho[ROWS - 1 : ROWS, :]
    edge_cols[0] = send1[0, 0, 0:1, :]
    edge_cols[1] = send1[1, NGX - 1, 7:8, :]
    load_weights.wait()
    row0_send[...] = weights[0:1, :]

    @pl.when(lax.rem(gy, 8) == 0)
    def _():
        row0_mid[...] = weights[0:1, :]

    pl.semaphore_wait(barrier, NGX - 1 + NGY - 1 + 1)

    def wrap(x, n):
        return jnp.where(x >= n, x - n, x)

    def far_first(t):
        return 4 - (t + 1) // 2 if t % 2 else 4 + t // 2

    def peer_gx(i):
        x = x_low if i // 16 else 1 - x_low
        y = wrap(y_at + far_first(i % 16 // 2), 8)
        return x * 16 + y * 2 + (core if i % 2 else 1 - core)

    def peer_gy(i):
        return wrap(z_at + far_first(i // 2), 8) * 2 + (x_high if i % 2 else 1 - x_high)

    def slot_of(y):
        q, b = y // 2, lax.rem(y, 2)
        return b * 8 + jnp.where(b == 0, q, 7 - q)

    def at(ref, where, start, size):
        return ref.at[(*where, pl.ds(pl.multiple_of(start, 8), size))]

    def ends(p, c, h, to):
        half = 16 * (x_low if h else 1 - x_low)
        if p == 0:
            return send1.at[c, to], recv1.at[c, gx]
        if p == 1:
            return at(send2, (c,), to * 16, 16), at(recv2, (c,), 256 * h + (gx - 16 * x_low) * 16, 16)
        if p == 2:
            return at(send3, (c,), 256 * h + slot_of(to) * 16, 16), at(recv3, (c,), gy * 32 + half, 16)
        if p == 3:
            return at(send4, (c,), to * 32 + half, 16), at(recv4, (c,), 256 * h + slot_of(gy) * 16, 16)
        if p == 4:
            there = x_low if h else 1 - x_low
            return at(send5, (c,), 256 * h + (to - 16 * there) * 16, 16), at(recv5, (c,), gx * 16, 16)
        return at(send6, (c,), to * 8, 8), recv6.at[pl.ds(pl.multiple_of(gx * 16 + 8 * c, 8), 8)]

    def message(p, c, h, i):
        over_gy = p in (2, 3)
        to = peer_gy(i) if over_gy else peer_gx(i + 16 * h)
        source, target = ends(p, c, h, to)
        return pltpu.make_async_remote_copy(
            src_ref=source, dst_ref=target, send_sem=send_sem.at[p, c], recv_sem=recv_sem.at[p, c, h],
            device_id={"gy" if over_gy else "gx": to}, device_id_type=MESH,
        )

    def count(p, h):
        return 16 if p not in (2, 3) and h == 0 else 15

    def own_copy(p, c, h):
        source, target = ends(p, c, h, gy if p in (2, 3) else gx)
        return pltpu.make_async_copy(source, target, local_sem.at[p, c, h])

    def start(p, c, h):
        for i in range(count(p, h)):
            message(p, c, h, i).start()
        if count(p, h) == 15:
            own_copy(p, c, h).start()

    def group(some, p, c, h):
        return pltpu.make_async_remote_copy(
            src_ref=some, dst_ref=some, send_sem=send_sem.at[p, c], recv_sem=recv_sem.at[p, c, h],
            device_id={"gx": lax.rem(gx + 1, NGX)}, device_id_type=MESH,
        )

    def finish(p, c, h):
        n = count(p, h)
        if n == 15:
            own_copy(p, c, h).wait()
        if p == 0:
            some = recv1.at[c, pl.ds(0, n)]
        elif p == 5:
            some = recv6.at[pl.ds(0, 8 * n)]
        else:
            some = (None, recv2, recv3, recv4, recv5)[p].at[c, pl.ds(0, 16 * n)]
        group(some, p, c, h).wait_recv()

    def sent(p, c):
        if p == 0:
            some = send1.at[c, pl.ds(0, 31)]
        elif p == 5:
            some = send6.at[c, pl.ds(0, 8 * 31)]
        else:
            some = (None, send2, send3, send4, send5)[p].at[c, pl.ds(0, 16 * (30 if p in (2, 3) else 31))]
        group(some, p, c, 0).wait_send()

    def halo(which, kind, k):
        axis, n, me = (("gx", NGX, gx), ("gy", NGY, gy))[kind]
        to = lax.rem(me + (n - 1 if k == 0 else 1), n)
        source, target = ((edge_rows, halo_rows), (edge_cols, halo_cols))[kind]
        return pltpu.make_async_remote_copy(
            src_ref=source.at[2 * which + k], dst_ref=target.at[2 * which + k],
            send_sem=halo_send.at[4 * which + 2 * kind + k], recv_sem=halo_recv.at[4 * which + 2 * kind + k],
            device_id={axis: to}, device_id_type=MESH,
        )

    def relay(source, target, k, where):
        return pltpu.make_async_remote_copy(
            src_ref=source, dst_ref=target, send_sem=k_send.at[k], recv_sem=k_recv.at[k], device_id=where,
            device_id_type=MESH,
        )

    weights_first = relay(weights.at[pl.ds(8, 8)], weights_mid, 0, across)
    weights_second = relay(weights_turned, weights_got, 1, {"gx": 32 * x_low + 15 - gx})

    def first_pieces(begin, end):
        for k in range(begin, end):
            lanes = pl.ds(1024 * k, 1024)
            relay(weights.at[pl.ds(8, 8), lanes], weights_mid.at[:, lanes], 0, across).start()

    def second_pieces(begin, end):
        for k in range(begin, end):
            rows = pl.ds(64 * k, 64)
            where = {"gx": 32 * x_low + 15 - gx}
            relay(weights_turned.at[rows], weights_got.at[rows], 1, where).start()

    row_first = relay(row0_send, row0_mid, 2, {"gy": lax.rem(NGY - gy, NGY)})
    edge_gx = jnp.where(gx == 0, 16, jnp.where(gx == 16, 0, lax.rem(NGX - gx, NGX)))
    row_second = relay(row0_mid, row0_got, 3, {"gx": jnp.where(gy == 0, edge_gx, NGX - 1 - gx)})
    row_moves = lower & (lax.rem(gy, 8) != 0)

    for c in range(2):
        for h in range(2):
            start(0, c, h)
            first_pieces(4 * c + 2 * h, 4 * c + 2 * h + 2)

    @pl.when(row_moves)
    def _():
        row_first.start()

    for kind in range(2):
        for k in range(2):
            halo(0, kind, k).start()

    wk[...] = direct_layout(jnp.where(lower, weights[1:9, :], weights[0:8, :]))

    @pl.when(row_moves)
    def _():
        row_first.wait_recv()

    @pl.when(lower)
    def _():
        row_second.start()

    ready("first", "twist_first", "second")
    first, second, twist_first = get("first"), get("second"), get("twist_first")[0]
    for c in range(2):
        finish(0, c, 0)
        finish(0, c, 1)
        x = recv1[c].reshape(256, 256)
        near_low, far_low, near_high, far_high = first_forward(
            x, [r[...] for r in first], twist_first, [r[...] for r in second]
        )
        for t in range(16):
            rows = slice(8 * t, 8 * t + 8)
            send2[c, 16 * t : 16 * t + 8] = near_low[rows]
            send2[c, 16 * (16 + t) : 16 * (16 + t) + 8] = near_high[rows]
            send2[c, 16 * (31 - t) + 8 : 16 * (31 - t) + 16] = far_low[rows]
            send2[c, 16 * (15 - t) + 8 : 16 * (15 - t) + 16] = far_high[rows]
        start(1, c, 0)
        start(1, c, 1)

    ready("flip", "order")
    flip = get("flip")[0][...]
    order_ref = get("order")[0]
    weights_first.wait_recv()

    @pl.when(jnp.logical_not(lower))
    def _():
        weights_mid[0:1, :] = jnp.zeros((1, N), F32)
        weights_turned[...] = mirror_layout(weights_mid[...], flip, order_ref[1])

    @pl.when(lower)
    def _():
        weights_turned[...] = mirror_layout(weights_mid[...], flip, order_ref[0])

    second_pieces(0, 2)

    @pl.when(jnp.logical_not(lower))
    def _():
        row_second.wait_recv()
        row = lax.broadcasted_iota(jnp.int32, (8, N), 0)

        @pl.when(device == 256)
        def _():
            one, two = weights[0:1, :], row0_got[...]
            only[...] = jnp.where(row == 0, jnp.broadcast_to(0.5 * (two - one), (8, N)), 0.0)
            change = direct_layout(only[...])
            wk[...] = wk[...] + change
            wk2[...] = change + mirror_layout(only[...], flip, order_ref[1])
            row0_got[...] = 0.5 * (one + two)

        only[...] = jnp.where(row == 0, jnp.broadcast_to(row0_got[...], (8, N)), 0.0)
        wk[...] = wk[...] + mirror_layout(only[...], flip, order_ref[1])

    for c in range(2):
        for h in range(2):
            finish(1, c, h)
            for slot in range(16):
                rows = slice(256 * h + 16 * slot, 256 * h + 16 * slot + 16)
                send3[c, rows] = recv2[c, pl.ds(256 * h + slot, 16, stride=16), :]
            start(2, c, h)
            second_pieces(2 + 2 * c + h, 8 if c + h == 2 else 3 + 2 * c + h)

    ready("c512", "s512", "twist_rows", "sixteen", "sixteen_back")
    c512, s512 = [r[...] for r in get("c512")], [r[...] for r in get("s512")]
    twist_rows, sixteen, sixteen_back = get("twist_rows")[0], get("sixteen"), get("sixteen_back")
    lane = lax.broadcasted_iota(jnp.int32, (1, 128), 1)
    sign = jnp.where(lane < 64, 1.0, -1.0)
    for c in range(2):
        lanes = slice(128 * c, 128 * c + 128)
        finish(2, c, 0)
        finish(2, c, 1)
        x = split(recv3[c])
        cosine, sine = mul(c512, x), mul(s512, x)
        co, si = twist_rows[0, :, lanes], twist_rows[1, :, lanes]
        one = co * cosine - si * sine
        two = -(si * cosine + co * sine)
        matrix = [r[c] for r in sixteen]
        part = mul(split(jnp.concatenate([one, two], axis=1)), matrix)
        spec[...] = part if c == 0 else spec[...] + part

        @pl.when(device == 256)
        def _():
            part = mul(split(jnp.concatenate([one * sign, two * sign], axis=1)), matrix)
            spec2[...] = part if c == 0 else spec2[...] + part

    weights_second.wait_recv()
    both_weights = wk[...] + weights_got[...]
    spec[:, :128] = spec[:, :128] * both_weights
    spec[:, 128:] = spec[:, 128:] * both_weights

    @pl.when(device == 256)
    def _():
        spec[:, :128] = spec[:, :128] + spec2[:, :128] * wk2[...]
        spec[:, 128:] = spec[:, 128:] + spec2[:, 128:] * wk2[...]

    prod = split(spec[...])
    for c in range(2):
        lanes = slice(128 * c, 128 * c + 128)
        u = mul(prod, [r[c] for r in sixteen_back])
        u, ui = u[:, :128], u[:, 128:]
        co, si = twist_rows[0, :, lanes], twist_rows[1, :, lanes]
        send4[c] = mul(c512, split(u * co + ui * si)) + mul(s512, split(ui * co - u * si))
        start(3, c, 0)
        start(3, c, 1)

    for c in range(2):
        for h in range(2):
            finish(3, c, h)
            for r in range(16):
                for b in range(2):
                    base = 256 * h + 16 * r + 8 * b
                    send5[c, base : base + 8] = recv4[c, pl.ds(256 * h + 128 * b + r, 8, stride=16), :]
            start(4, c, h)

    ready("second_back", "twist_last", "last")
    second_back = [r[...] for r in get("second_back")]
    twist_last = get("twist_last")[0]
    last = [r[...] for r in get("last")]
    for c in range(2):
        finish(4, c, 0)
        finish(4, c, 1)
        near = [recv5[c, 16 * t : 16 * t + 8] for t in range(32)]
        far = [recv5[c, 16 * (31 - t) + 8 : 16 * (31 - t) + 16] for t in range(32)]
        near, far = jnp.concatenate(near, axis=0), jnp.concatenate(far, axis=0)
        both = jnp.concatenate([near, far], axis=1)
        send6[c] = first_inverse(both[:128], both[128:], second_back, twist_last, last)
        start(5, c, 0)
        start(5, c, 1)

    padded_rho[8 : 8 + ROWS, :] = rho[...]
    for kind in range(2):
        for k in range(2):
            halo(0, kind, k).wait_recv()
    padded_rho[7:8, :] = halo_rows[1]
    padded_rho[8 + ROWS : 9 + ROWS, :] = halo_rows[0]
    for c in range(2):
        for h in range(2):
            finish(5, c, h)
    edge_cols[2] = recv6[0:1, :]
    edge_cols[3] = recv6[COLS - 1 : COLS, :]
    for k in range(2):
        halo(1, 1, k).start()
    for b in range(4):
        padded_pot[8 : 8 + ROWS, 128 * b : 128 * b + 128] = recv6[128 * b : 128 * b + 128, :].T
    edge_rows[2] = padded_pot[8:9, :]
    edge_rows[3] = padded_pot[7 + ROWS : 8 + ROWS, :]
    for k in range(2):
        halo(1, 0, k).start()
    pot_out[...] = 0.5 * padded_pot[8 : 8 + ROWS, :]
    pot_store = pltpu.make_async_copy(pot_out, pot_ref, load_sem.at[2])
    pot_store.start()
    for k in range(2):
        halo(1, 1, k).wait_recv()
    columns = jnp.concatenate([halo_cols[k] for k in range(4)] + [jnp.zeros((4, ROWS), F32)], axis=0).T
    lane = lax.broadcasted_iota(jnp.int32, (32, COLS), 1)
    for block in (1, 2, 3, 4, 5, 6, 0, 7):
        if block == 0:
            for k in range(2):
                halo(1, 0, k).wait_recv()
            padded_pot[7:8, :] = halo_rows[3]
            padded_pot[8 + ROWS : 9 + ROWS, :] = halo_rows[2]
        base = 8 + 32 * block
        r, p = padded_rho[base : base + 32, :], padded_pot[base : base + 32, :]
        cols = columns[32 * block : 32 * block + 32]
        above = face_flux(r, padded_rho[base + 1 : base + 33, :], p, padded_pot[base + 1 : base + 33, :])
        below = face_flux(padded_rho[base - 1 : base + 31, :], r, padded_pot[base - 1 : base + 31, :], p)
        r_next = jnp.where(lane == COLS - 1, cols[:, 0:1], pltpu.roll(r, COLS - 1, 1))
        p_next = jnp.where(lane == COLS - 1, cols[:, 2:3], pltpu.roll(p, COLS - 1, 1))
        right = face_flux(r, r_next, p, p_next)
        r_edge = jnp.broadcast_to(cols[:, 1:2], (32, 128))
        p_edge = jnp.broadcast_to(cols[:, 3:4], (32, 128))
        first_left = face_flux(r_edge, r[:, :128], p_edge, p[:, :128])[:, 0:1]
        left = jnp.where(lane == 0, first_left, pltpu.roll(right, 1, 1))
        change = TIME_STEP * ((above - below) + (right - left))
        new_out[32 * block : 32 * block + 32, :] = 0.5 * (r - change)
    new_store = pltpu.make_async_copy(new_out, new_ref, load_sem.at[3])
    new_store.start()

    for p in range(6):
        for c in range(2):
            sent(p, c)
    for which in range(2):
        for kind in range(2):
            for k in range(2):
                halo(which, kind, k).wait_send()
    weights_first.wait_send()
    weights_second.wait_send()

    @pl.when(row_moves)
    def _():
        row_first.wait_send()

    @pl.when(lower)
    def _():
        row_second.wait_send()

    pot_store.wait()
    new_store.wait()


def local(density, kernel_hat):
    constants, index = flat_constants()
    pieces, packs = pack(constants)
    vmem = lambda *shape: pltpu.VMEM(shape, F32)
    dma = lambda *shape: pltpu.SemaphoreType.DMA(shape)
    n_const = len(constants)
    scratch = [pltpu.VMEM(c.shape, c.dtype) for c in constants] + [
        vmem(ROWS, COLS), vmem(16, N), vmem(8, N), vmem(512, 128), vmem(512, 128), vmem(1, N), vmem(1, N), vmem(1, N), vmem(8, N),
        vmem(512, 128), vmem(512, 128), vmem(512, 256), vmem(512, 256),
        vmem(2, 32, 8, 256), vmem(2, 32, 8, 256),
        vmem(2, 512, 128), vmem(2, 512, 128), vmem(2, 512, 128), vmem(2, 512, 128),
        vmem(2, 512, 128), vmem(2, 512, 128), vmem(2, 512, 128), vmem(2, 512, 128),
        vmem(2, 256, 256), vmem(512, 256),
        vmem(4, 1, COLS), vmem(4, 1, ROWS), vmem(4, 1, COLS), vmem(4, 1, ROWS),
        vmem(ROWS + 16, COLS), vmem(ROWS + 16, COLS), vmem(ROWS, COLS), vmem(ROWS, COLS),
        dma(6, 2), dma(6, 2, 2), dma(6, 2, 2), dma(4), dma(len(pieces)), dma(4), dma(4), dma(8), dma(8),
    ]
    out = jax.ShapeDtypeStruct((ROWS, COLS), F32)
    half_potential, half_density = pl.pallas_call(
        functools.partial(kernel, index, n_const, pieces),
        out_shape=(out, out),
        in_specs=[pl.BlockSpec(memory_space=pl.ANY)] * 4,
        out_specs=(pl.BlockSpec(memory_space=pl.ANY),) * 2,
        scratch_shapes=scratch,
        compiler_params=pltpu.CompilerParams(
            collective_id=0, has_side_effects=True, vmem_limit_bytes=52 * 1024 * 1024
        ),
        name="convolve_step",
    )(density, kernel_hat, *[jnp.asarray(p) for p in packs])
    return 2.0 * half_potential, 2.0 * half_density


def solution(mesh):
    return jax.shard_map(
        local, mesh=mesh, in_specs=(P("gx", "gy"), P(("gx", "gy"), None)),
        out_specs=(P("gx", "gy"), P("gx", "gy")), check_vma=False,
    )
```

```python
import functools

import jax
import jax.numpy as jnp
import numpy as np
from jax import lax
from jax.experimental import pallas as pl
from jax.experimental.pallas import tpu as pltpu
from jax.sharding import PartitionSpec as P

TIME_STEP = 0.2
DIFFUSION = 0.25
MESH = pl.DeviceIdType.MESH
F32, BF16 = jnp.float32, jnp.bfloat16
NGX, NGY, N = 32, 16, 8192
ROWS, COLS = 256, 512


def split_np(table):
    table = np.asarray(table, np.float32)
    high = table.astype(BF16)
    low = (table - high.astype(np.float32)).astype(BF16)
    return high, low


def angle(a, b, modulus):
    product = np.asarray(a, np.int64) * np.asarray(b, np.int64) % modulus
    return 2.0 * np.pi * product / modulus


def slot_frequency(half, side, j):
    if half == 0:
        return j + 1 if side == 0 else 16 - j
    return j if side == 0 else 15 - j


@functools.lru_cache(maxsize=None)
def tables():
    t = {}
    eye8 = np.eye(8)
    g = np.arange(32)
    slots = np.arange(16)
    real_rows = np.cos(angle(slots[:, None], g[None], 32))
    imag_rows = -np.sin(angle(slots[:, None], g[None], 32))
    imag_rows[0] = np.cos(angle(16, g, 32))
    t["first"] = split_np(np.kron(np.concatenate([real_rows, imag_rows]), eye8))
    m = np.arange(256)
    theta = angle(slots[:, None], m[None], N)
    last = angle(16, m, N)
    ca, sa, cb, sb = np.cos(theta), np.sin(theta), np.cos(theta), np.sin(theta)
    ca[0], sa[0], cb[0], sb[0] = 0.0, np.cos(last), -np.sin(last), 0.0
    t["twist_first"] = np.repeat(np.stack([ca, sa, cb, sb]), 8, axis=1).astype(np.float32)
    w256 = angle(m[:, None], m[None], 256)
    c256, s256 = np.cos(w256), np.sin(w256)
    forward = np.concatenate([c256, s256], axis=1)
    ones = np.zeros((16, 512))
    ones[0, :256] = 1.0
    t["second"] = split_np(np.concatenate([forward[:128], forward[128:], ones]))
    a = np.arange(512)
    w512 = angle(a[:, None], a[None], 512)
    t["c512"] = split_np(np.cos(w512))
    t["s512"] = split_np(np.sin(w512))
    lane = np.arange(256)
    l16 = 8 * (lane // 128) + lane % 8
    theta = angle(a[:, None], l16[None], N)
    t["twist_rows"] = np.stack([np.cos(theta), np.sin(theta)]).astype(np.float32)
    lin = np.arange(16)
    phi = angle(lin[:, None], lin[None], 16)

    def embed(sign):
        out = np.zeros((2, 2, 8, 8, 2, 16, 8))
        for c in range(2):
            for l8 in range(8):
                co, si = np.cos(phi[8 * c + l8]), sign * np.sin(phi[8 * c + l8])
                for j in range(8):
                    out[c, 0, j, l8, 0, :, j] = co
                    out[c, 0, j, l8, 1, :, j] = si
                    out[c, 1, j, l8, 0, :, j] = -si
                    out[c, 1, j, l8, 1, :, j] = co
        return out.reshape(256, 256)

    def times_i_rows(matrix):
        parts = matrix.reshape(2, 2, 64, -1)
        return np.stack([parts[:, 1], -parts[:, 0]], axis=1).reshape(matrix.shape)

    m2 = embed(-1.0)
    both = np.stack([m2, times_i_rows(m2)]).reshape(2, 2, 128, 256).transpose(1, 0, 2, 3)
    t["sixteen"] = split_np(both.reshape(2, 256, 256))
    inv = np.zeros((2, 16, 8, 2, 2, 8, 8))
    for c in range(2):
        for l8 in range(8):
            co, si = np.cos(phi[8 * c + l8]), np.sin(phi[8 * c + l8])
            for j in range(8):
                inv[0, :, j, c, 0, j, l8] = co
                inv[0, :, j, c, 1, j, l8] = si
                inv[1, :, j, c, 0, j, l8] = -si
                inv[1, :, j, c, 1, j, l8] = co
    turned = np.zeros_like(inv)
    turned[:, :, :, :, 0] = -inv[:, :, :, :, 1]
    turned[:, :, :, :, 1] = inv[:, :, :, :, 0]
    both = np.stack([inv.reshape(256, 2, 128), turned.reshape(256, 2, 128)], axis=2)
    t["sixteen_back"] = split_np(both.transpose(1, 0, 2, 3).reshape(2, 256, 256))
    t["second_back"] = split_np(
        np.concatenate([np.concatenate([c256[:, h], s256[:, h]]) for h in (slice(0, 128), slice(128, 256))])
    )
    freq = np.zeros((2, 2, 2, 8, 8), np.int64)
    for half in range(2):
        for side in range(2):
            for j in range(8):
                freq[half, side, :, j, :] = slot_frequency(half, side, j)
    flat = freq.reshape(2, 256)
    theta = angle(m[None, :, None], flat[:, None, :], N)
    t["twist_last"] = np.stack([np.cos(theta), np.sin(theta)], axis=1).reshape(4, 256, 256).astype(np.float32)
    last = np.zeros((32, 8, 2, 2, 2, 2, 8, 8))
    scale = 2.0 / (float(N) * float(N))
    for half in range(2):
        for side in range(2):
            conj = 1.0 if side == 0 else -1.0
            for j in range(8):
                arc = angle(g, slot_frequency(half, side, j), 32)
                for l in range(8):
                    last[:, l, half, 0, side, 0, j, l] = scale * np.cos(arc)
                    last[:, l, half, 0, side, 1, j, l] = -scale * np.sin(arc) * conj
                    last[:, l, half, 1, side, 0, j, l] = -scale * np.sin(arc)
                    last[:, l, half, 1, side, 1, j, l] = -scale * np.cos(arc) * conj
    t["last"] = split_np(last.reshape(256, 1024))
    flip = np.zeros((512, 512))
    flip[a, (-a) % 512] = 1.0
    t["flip"] = flip.astype(BF16)
    order = np.zeros((2, 16, 8, 16, 8))
    for kb in range(16):
        for s in range(8):
            order[0, kb, s, kb, 7 - s] = 1.0
            order[1, kb, s, kb, (8 - s) % 8] = 1.0
    t["order"] = order.reshape(2, 128, 128).astype(BF16)
    return t


def split(x):
    high = x.astype(BF16)
    return high, (x - high.astype(F32)).astype(BF16)


def mul(a, b, transposed=False):
    dims = (((1,), (1 if transposed else 0,)), ((), ()))
    dot = lambda x, y: lax.dot_general(x, y, dims, preferred_element_type=F32)
    return dot(a[0], b[0]) + (dot(a[0], b[1]) + dot(a[1], b[0]))


def mul_exact(selector, x, transposed=False):
    dims = (((1,), (1 if transposed else 0,)), ((), ()))
    dot = lambda p, q: lax.dot_general(p, q, dims, preferred_element_type=F32)
    high, low = split(x)
    return dot(selector, high) + dot(selector, low)


def first_forward(x, first, twist, second):
    spun = mul(first, split(x))
    real, imag = spun[:128], spun[128:]
    plain = real[:8]
    turned_real = real * twist[0] + imag * twist[1]
    turned_imag = imag * twist[2] - real * twist[3]

    def rows(table, order):
        return [table[8 * s : 8 * s + 8] for s in order]

    outs = []
    for half in range(2):
        if half == 0:
            near, far = list(range(1, 9)), [0] + list(range(15, 8, -1))
            re, im = turned_real, turned_imag
        else:
            near, far = list(range(8)), list(range(15, 7, -1))
            re = jnp.concatenate([plain, turned_real[8:]], axis=0)
            im = jnp.concatenate([jnp.zeros_like(plain), turned_imag[8:]], axis=0)
        cosine = jnp.concatenate(rows(re, near) + rows(im, near) + rows(re, far) + rows(-im, far), axis=0)
        sine = jnp.concatenate(rows(im, near) + rows(-re, near) + rows(im, far) + rows(re, far), axis=0)
        cosine, sine = split(cosine), split(sine)
        picked = slice(0, 128) if half == 0 else slice(128, 272)
        w = [v[picked] for v in second]
        out = mul([v[:, :256] for v in w], cosine, True) + mul([v[:, 256:] for v in w], sine, True)
        outs.append(out)
    low, high = outs[0], outs[1][:128]
    total = outs[1][128:136, :128]
    tile = high[:8, :128]
    row = lax.broadcasted_iota(jnp.int32, (8, 128), 0)
    lane = lax.broadcasted_iota(jnp.int32, (8, 128), 1)
    tile = jnp.where((row == 0) & (lane >= 64) & (lane < 72), pltpu.roll(tile, 64, 1), tile)
    tile = jnp.where((row == 0) & (lane < 8), total, tile)
    near_high = jnp.concatenate([tile, high[8:, :128]], axis=0)
    return low[:, :128], low[:, 128:], near_high, high[:, 128:]


def first_inverse(low, high, second_back, twist, last):
    row = lax.broadcasted_iota(jnp.int32, (8, 128), 0)
    lane = lax.broadcasted_iota(jnp.int32, (8, 128), 1)
    tile = high[:8, :128]
    constant = jnp.where(lane < 8, 0.5 * tile, 0.0)[:1]
    other = jnp.where(lane < 8, 0.5 * pltpu.roll(tile, 64, 1), jnp.where((lane >= 64) & (lane < 72), 0.0, tile))
    tile = jnp.where(row == 0, other, tile)
    top = jnp.concatenate([tile, high[:8, 128:]], axis=1)
    high = jnp.concatenate([top, high[8:]], axis=0)
    total = None
    for half, x in ((0, low), (1, high)):
        spun = mul([v[512 * half : 512 * half + 512] for v in second_back], split(x))
        cosine, sine = spun[:256], spun[256:]
        if half == 1:
            cosine = jnp.concatenate([cosine[:, :128] + constant, cosine[:, 128:]], axis=1)
        co, si = twist[2 * half], twist[2 * half + 1]
        one = co * cosine - si * sine
        two = si * cosine + co * sine
        for k, part in ((0, one), (1, two)):
            at = 512 * half + 256 * k
            term = mul([v[:, at : at + 256] for v in last], split(part), True)
            total = term if total is None else total + term
    return total


def face_flux(lower_rho, upper_rho, lower_pot, upper_pot):
    speed = lower_pot - upper_pot
    drift = jnp.maximum(speed, 0.0) * lower_rho * (1.0 - upper_rho) + jnp.minimum(speed, 0.0) * upper_rho * (
        1.0 - lower_rho
    )
    return drift + DIFFUSION * (lower_rho * lower_rho - upper_rho * upper_rho)


def direct_layout(own):
    return 0.5 * jnp.concatenate([own[:, 512 * b : 512 * b + 512] for b in range(16)], axis=0).T


def mirror_layout(other, flip, order):
    mirror = jnp.concatenate([other[:, 512 * (15 - b) : 512 * (15 - b) + 512] for b in range(16)], axis=0)
    turned = mul_exact(flip, mirror, True)
    top = turned[:8]
    row = lax.broadcasted_iota(jnp.int32, (8, 128), 0)
    top = jnp.where(row == 0, pltpu.roll(top, 8, 1), top)
    turned = jnp.concatenate([top, turned[8:]], axis=0)
    high, low = split(turned)
    dot = lambda x: jnp.dot(x, order, preferred_element_type=F32)
    return 0.5 * (dot(high) + dot(low))


CONSTANTS = (
    "first", "twist_first", "second", "c512", "s512", "twist_rows", "sixteen", "sixteen_back",
    "second_back", "twist_last", "last", "flip", "order",
)


def flat_constants():
    out, index = [], {}
    for name in CONSTANTS:
        value = tables()[name]
        value = value if isinstance(value, tuple) else (value,)
        index[name] = list(range(len(out), len(out) + len(value)))
        out.extend(value)
    return out, index


def pack(values):
    pieces, stacks = [], ([], [])
    for i, value in enumerate(values):
        which = 0 if value.dtype == np.float32 else 1
        planes = value if value.ndim == 3 else value[None]
        for k, plane in enumerate(planes):
            begin = sum(p.shape[0] for p in stacks[which])
            pieces.append((i, k if value.ndim == 3 else None, which, begin, *plane.shape))
            stacks[which].append(np.pad(plane, ((0, 0), (0, 1024 - plane.shape[1]))))
    return pieces, [np.concatenate(stack) for stack in stacks]


def kernel(index, n_const, pieces, *refs):
    rho_ref, kernel_ref = refs[:2]
    packs = refs[2:4]
    pot_ref, new_ref = refs[4:6]
    rest = list(refs[6:])
    const = [rest.pop(0) for _ in range(n_const)]
    (
        rho, weights, weights_mid, weights_turned, weights_got, row0_send, row0_mid, row0_got, only, wk, wk2, spec, spec2,
        send1, recv1, send2, recv2, send3, recv3, send4, recv4, send5, recv5, send6, recv6,
        edge_rows, edge_cols, halo_rows, halo_cols, padded_rho, padded_pot, pot_out, new_out,
        send_sem, recv_sem, local_sem, load_sem, const_sem, k_send, k_recv, halo_send, halo_recv,
    ) = rest
    gx, gy = lax.axis_index("gx"), lax.axis_index("gy")
    x_low, y_at, core = gx // 16, lax.rem(gx // 2, 8), lax.rem(gx, 2)
    z_at, x_high = gy // 2, lax.rem(gy, 2)
    device = gx * NGY + gy
    lower = gx < NGX // 2

    def get(name):
        return [const[i] for i in index[name]]

    barrier = pltpu.get_barrier_semaphore()

    def greet(axis, n, me):
        def body(i, carry):
            pl.semaphore_signal(barrier, inc=1, device_id={axis: lax.rem(me + i, n)}, device_id_type=MESH)
            return carry

        lax.fori_loop(1, n, body, 0)

    across = {"gx": gx + 16 - 32 * x_low, "gy": NGY - 1 - gy}
    pl.semaphore_signal(barrier, inc=1, device_id=across, device_id_type=MESH)
    greet("gx", NGX, gx)
    greet("gy", NGY, gy)

    load_rho = pltpu.make_async_copy(rho_ref, rho, load_sem.at[0])
    load_weights = pltpu.make_async_copy(kernel_ref, weights, load_sem.at[1])
    load_rho.start()
    load_weights.start()
    loads = [[] for _ in range(n_const)]
    for at_piece, (i, k, which, begin, rows, width) in enumerate(pieces):
        source = packs[which].at[pl.ds(begin, rows), pl.ds(0, width)]
        target = const[i] if k is None else const[i].at[k]
        load = pltpu.make_async_copy(source, target, const_sem.at[at_piece])
        load.start()
        loads[i].append(load)

    def ready(*names):
        for name in names:
            for i in index[name]:
                for load in loads[i]:
                    load.wait()

    load_rho.wait()
    for b in range(4):
        turned = rho[:, 128 * b : 128 * b + 128].T
        for part in range(8):
            for c in range(2):
                send1[c, 8 * b + part] = turned[16 * part + 8 * c : 16 * part + 8 * c + 8]
    edge_rows[0] = rho[0:1, :]
    edge_rows[1] = rho[ROWS - 1 : ROWS, :]
    edge_cols[0] = send1[0, 0, 0:1, :]
    edge_cols[1] = send1[1, NGX - 1, 7:8, :]
    load_weights.wait()
    row0_send[...] = weights[0:1, :]

    @pl.when(lax.rem(gy, 8) == 0)
    def _():
        row0_mid[...] = weights[0:1, :]

    pl.semaphore_wait(barrier, NGX - 1 + NGY - 1 + 1)

    def wrap(x, n):
        return jnp.where(x >= n, x - n, x)

    def far_first(t):
        return 4 - (t + 1) // 2 if t % 2 else 4 + t // 2

    def peer_gx(i):
        x = x_low if i // 16 else 1 - x_low
        y = wrap(y_at + far_first(i % 16 // 2), 8)
        return x * 16 + y * 2 + (core if i % 2 else 1 - core)

    def peer_gy(i):
        return wrap(z_at + far_first(i // 2), 8) * 2 + (x_high if i % 2 else 1 - x_high)

    def slot_of(y):
        q, b = y // 2, lax.rem(y, 2)
        return b * 8 + jnp.where(b == 0, q, 7 - q)

    def at(ref, where, start, size):
        return ref.at[(*where, pl.ds(pl.multiple_of(start, 8), size))]

    def ends(p, c, h, to):
        half = 16 * (x_low if h else 1 - x_low)
        if p == 0:
            return send1.at[c, to], recv1.at[c, gx]
        if p == 1:
            return at(send2, (c,), to * 16, 16), at(recv2, (c,), 256 * h + (gx - 16 * x_low) * 16, 16)
        if p == 2:
            return at(send3, (c,), 256 * h + slot_of(to) * 16, 16), at(recv3, (c,), gy * 32 + half, 16)
        if p == 3:
            return at(send4, (c,), to * 32 + half, 16), at(recv4, (c,), 256 * h + slot_of(gy) * 16, 16)
        if p == 4:
            there = x_low if h else 1 - x_low
            return at(send5, (c,), 256 * h + (to - 16 * there) * 16, 16), at(recv5, (c,), gx * 16, 16)
        return at(send6, (c,), to * 8, 8), recv6.at[pl.ds(pl.multiple_of(gx * 16 + 8 * c, 8), 8)]

    def message(p, c, h, i):
        over_gy = p in (2, 3)
        to = peer_gy(i) if over_gy else peer_gx(i + 16 * h)
        source, target = ends(p, c, h, to)
        return pltpu.make_async_remote_copy(
            src_ref=source, dst_ref=target, send_sem=send_sem.at[p, c], recv_sem=recv_sem.at[p, c, h],
            device_id={"gy" if over_gy else "gx": to}, device_id_type=MESH,
        )

    def count(p, h):
        return 16 if p not in (2, 3) and h == 0 else 15

    def own_copy(p, c, h):
        source, target = ends(p, c, h, gy if p in (2, 3) else gx)
        return pltpu.make_async_copy(source, target, local_sem.at[p, c, h])

    def start(p, c, h):
        for i in range(count(p, h)):
            message(p, c, h, i).start()
        if count(p, h) == 15:
            own_copy(p, c, h).start()

    def group(some, p, c, h):
        return pltpu.make_async_remote_copy(
            src_ref=some, dst_ref=some, send_sem=send_sem.at[p, c], recv_sem=recv_sem.at[p, c, h],
            device_id={"gx": lax.rem(gx + 1, NGX)}, device_id_type=MESH,
        )

    def finish(p, c, h):
        n = count(p, h)
        if n == 15:
            own_copy(p, c, h).wait()
        if p == 0:
            some = recv1.at[c, pl.ds(0, n)]
        elif p == 5:
            some = recv6.at[pl.ds(0, 8 * n)]
        else:
            some = (None, recv2, recv3, recv4, recv5)[p].at[c, pl.ds(0, 16 * n)]
        group(some, p, c, h).wait_recv()

    def sent(p, c):
        if p == 0:
            some = send1.at[c, pl.ds(0, 31)]
        elif p == 5:
            some = send6.at[c, pl.ds(0, 8 * 31)]
        else:
            some = (None, send2, send3, send4, send5)[p].at[c, pl.ds(0, 16 * (30 if p in (2, 3) else 31))]
        group(some, p, c, 0).wait_send()

    def halo(which, kind, k):
        axis, n, me = (("gx", NGX, gx), ("gy", NGY, gy))[kind]
        to = lax.rem(me + (n - 1 if k == 0 else 1), n)
        source, target = ((edge_rows, halo_rows), (edge_cols, halo_cols))[kind]
        return pltpu.make_async_remote_copy(
            src_ref=source.at[2 * which + k], dst_ref=target.at[2 * which + k],
            send_sem=halo_send.at[4 * which + 2 * kind + k], recv_sem=halo_recv.at[4 * which + 2 * kind + k],
            device_id={axis: to}, device_id_type=MESH,
        )

    def relay(source, target, k, where):
        return pltpu.make_async_remote_copy(
            src_ref=source, dst_ref=target, send_sem=k_send.at[k], recv_sem=k_recv.at[k], device_id=where,
            device_id_type=MESH,
        )

    weights_first = relay(weights.at[pl.ds(8, 8)], weights_mid, 0, across)
    weights_second = relay(weights_turned, weights_got, 1, {"gx": 32 * x_low + 15 - gx})

    def first_pieces(begin, end):
        for k in range(begin, end):
            lanes = pl.ds(1024 * k, 1024)
            relay(weights.at[pl.ds(8, 8), lanes], weights_mid.at[:, lanes], 0, across).start()

    def second_pieces(begin, end):
        for k in range(begin, end):
            rows = pl.ds(64 * k, 64)
            where = {"gx": 32 * x_low + 15 - gx}
            relay(weights_turned.at[rows], weights_got.at[rows], 1, where).start()

    row_first = relay(row0_send, row0_mid, 2, {"gy": lax.rem(NGY - gy, NGY)})
    edge_gx = jnp.where(gx == 0, 16, jnp.where(gx == 16, 0, lax.rem(NGX - gx, NGX)))
    row_second = relay(row0_mid, row0_got, 3, {"gx": jnp.where(gy == 0, edge_gx, NGX - 1 - gx)})
    row_moves = lower & (lax.rem(gy, 8) != 0)

    for c in range(2):
        for h in range(2):
            start(0, c, h)
            first_pieces(4 * c + 2 * h, 4 * c + 2 * h + 2)

    @pl.when(row_moves)
    def _():
        row_first.start()

    for kind in range(2):
        for k in range(2):
            halo(0, kind, k).start()

    wk[...] = direct_layout(jnp.where(lower, weights[1:9, :], weights[0:8, :]))

    @pl.when(row_moves)
    def _():
        row_first.wait_recv()

    @pl.when(lower)
    def _():
        row_second.start()

    ready("first", "twist_first", "second")
    first, second, twist_first = get("first"), get("second"), get("twist_first")[0]
    for c in range(2):
        finish(0, c, 0)
        finish(0, c, 1)
        x = recv1[c].reshape(256, 256)
        near_low, far_low, near_high, far_high = first_forward(
            x, [r[...] for r in first], twist_first, [r[...] for r in second]
        )
        for t in range(16):
            rows = slice(8 * t, 8 * t + 8)
            send2[c, 16 * t : 16 * t + 8] = near_low[rows]
            send2[c, 16 * (16 + t) : 16 * (16 + t) + 8] = near_high[rows]
            send2[c, 16 * (31 - t) + 8 : 16 * (31 - t) + 16] = far_low[rows]
            send2[c, 16 * (15 - t) + 8 : 16 * (15 - t) + 16] = far_high[rows]
        start(1, c, 0)
        start(1, c, 1)

    def relay_weights():
        ready("flip", "order")
        flip = get("flip")[0][...]
        order_ref = get("order")[0]
        weights_first.wait_recv()

        @pl.when(jnp.logical_not(lower))
        def _():
            weights_mid[0:1, :] = jnp.zeros((1, N), F32)
            weights_turned[...] = mirror_layout(weights_mid[...], flip, order_ref[1])

        @pl.when(lower)
        def _():
            weights_turned[...] = mirror_layout(weights_mid[...], flip, order_ref[0])

        second_pieces(0, 4)

        @pl.when(jnp.logical_not(lower))
        def _():
            row_second.wait_recv()
            row = lax.broadcasted_iota(jnp.int32, (8, N), 0)

            @pl.when(device == 256)
            def _():
                one, two = weights[0:1, :], row0_got[...]
                only[...] = jnp.where(row == 0, jnp.broadcast_to(0.5 * (two - one), (8, N)), 0.0)
                change = direct_layout(only[...])
                wk[...] = wk[...] + change
                wk2[...] = change + mirror_layout(only[...], flip, order_ref[1])
                row0_got[...] = 0.5 * (one + two)

            only[...] = jnp.where(row == 0, jnp.broadcast_to(row0_got[...], (8, N)), 0.0)
            wk[...] = wk[...] + mirror_layout(only[...], flip, order_ref[1])

    for c in range(2):
        if c == 1:
            relay_weights()
        for h in range(2):
            finish(1, c, h)
            for slot in range(16):
                rows = slice(256 * h + 16 * slot, 256 * h + 16 * slot + 16)
                send3[c, rows] = recv2[c, pl.ds(256 * h + slot, 16, stride=16), :]
            start(2, c, h)
            if c == 1:
                second_pieces(4 + 2 * h, 6 + 2 * h)

    ready("c512", "s512", "twist_rows", "sixteen", "sixteen_back")
    c512, s512 = [r[...] for r in get("c512")], [r[...] for r in get("s512")]
    twist_rows, sixteen, sixteen_back = get("twist_rows")[0], get("sixteen"), get("sixteen_back")
    lane = lax.broadcasted_iota(jnp.int32, (1, 128), 1)
    sign = jnp.where(lane < 64, 1.0, -1.0)
    for c in range(2):
        lanes = slice(128 * c, 128 * c + 128)
        finish(2, c, 0)
        finish(2, c, 1)
        x = split(recv3[c])
        cosine, sine = mul(c512, x), mul(s512, x)
        co, si = twist_rows[0, :, lanes], twist_rows[1, :, lanes]
        one = co * cosine - si * sine
        two = -(si * cosine + co * sine)
        matrix = [r[c] for r in sixteen]
        part = mul(split(jnp.concatenate([one, two], axis=1)), matrix)
        spec[...] = part if c == 0 else spec[...] + part

        @pl.when(device == 256)
        def _():
            part = mul(split(jnp.concatenate([one * sign, two * sign], axis=1)), matrix)
            spec2[...] = part if c == 0 else spec2[...] + part

    weights_second.wait_recv()
    both_weights = wk[...] + weights_got[...]
    spec[:, :128] = spec[:, :128] * both_weights
    spec[:, 128:] = spec[:, 128:] * both_weights

    @pl.when(device == 256)
    def _():
        spec[:, :128] = spec[:, :128] + spec2[:, :128] * wk2[...]
        spec[:, 128:] = spec[:, 128:] + spec2[:, 128:] * wk2[...]

    prod = split(spec[...])
    for c in range(2):
        lanes = slice(128 * c, 128 * c + 128)
        u = mul(prod, [r[c] for r in sixteen_back])
        u, ui = u[:, :128], u[:, 128:]
        co, si = twist_rows[0, :, lanes], twist_rows[1, :, lanes]
        send4[c] = mul(c512, split(u * co + ui * si)) + mul(s512, split(ui * co - u * si))
        start(3, c, 0)
        start(3, c, 1)

    for c in range(2):
        for h in range(2):
            finish(3, c, h)
            for r in range(16):
                for b in range(2):
                    base = 256 * h + 16 * r + 8 * b
                    send5[c, base : base + 8] = recv4[c, pl.ds(256 * h + 128 * b + r, 8, stride=16), :]
            start(4, c, h)

    ready("second_back", "twist_last", "last")
    second_back = [r[...] for r in get("second_back")]
    twist_last = get("twist_last")[0]
    last = [r[...] for r in get("last")]
    for c in range(2):
        finish(4, c, 0)
        finish(4, c, 1)
        near = [recv5[c, 16 * t : 16 * t + 8] for t in range(32)]
        far = [recv5[c, 16 * (31 - t) + 8 : 16 * (31 - t) + 16] for t in range(32)]
        near, far = jnp.concatenate(near, axis=0), jnp.concatenate(far, axis=0)
        both = jnp.concatenate([near, far], axis=1)
        send6[c] = first_inverse(both[:128], both[128:], second_back, twist_last, last)
        start(5, c, 0)
        start(5, c, 1)

    padded_rho[8 : 8 + ROWS, :] = rho[...]
    for kind in range(2):
        for k in range(2):
            halo(0, kind, k).wait_recv()
    padded_rho[7:8, :] = halo_rows[1]
    padded_rho[8 + ROWS : 9 + ROWS, :] = halo_rows[0]
    for c in range(2):
        for h in range(2):
            finish(5, c, h)
    edge_cols[2] = recv6[0:1, :]
    edge_cols[3] = recv6[COLS - 1 : COLS, :]
    for k in range(2):
        halo(1, 1, k).start()
    for b in range(4):
        padded_pot[8 : 8 + ROWS, 128 * b : 128 * b + 128] = recv6[128 * b : 128 * b + 128, :].T
    edge_rows[2] = padded_pot[8:9, :]
    edge_rows[3] = padded_pot[7 + ROWS : 8 + ROWS, :]
    for k in range(2):
        halo(1, 0, k).start()
    pot_out[...] = 0.5 * padded_pot[8 : 8 + ROWS, :]
    pot_store = pltpu.make_async_copy(pot_out, pot_ref, load_sem.at[2])
    pot_store.start()
    for k in range(2):
        halo(1, 1, k).wait_recv()
    columns = jnp.concatenate([halo_cols[k] for k in range(4)] + [jnp.zeros((4, ROWS), F32)], axis=0).T
    lane = lax.broadcasted_iota(jnp.int32, (32, COLS), 1)
    for block in (1, 2, 3, 4, 5, 6, 0, 7):
        if block == 0:
            for k in range(2):
                halo(1, 0, k).wait_recv()
            padded_pot[7:8, :] = halo_rows[3]
            padded_pot[8 + ROWS : 9 + ROWS, :] = halo_rows[2]
        base = 8 + 32 * block
        r, p = padded_rho[base : base + 32, :], padded_pot[base : base + 32, :]
        cols = columns[32 * block : 32 * block + 32]
        above = face_flux(r, padded_rho[base + 1 : base + 33, :], p, padded_pot[base + 1 : base + 33, :])
        below = face_flux(padded_rho[base - 1 : base + 31, :], r, padded_pot[base - 1 : base + 31, :], p)
        r_next = jnp.where(lane == COLS - 1, cols[:, 0:1], pltpu.roll(r, COLS - 1, 1))
        p_next = jnp.where(lane == COLS - 1, cols[:, 2:3], pltpu.roll(p, COLS - 1, 1))
        right = face_flux(r, r_next, p, p_next)
        r_edge = jnp.broadcast_to(cols[:, 1:2], (32, 128))
        p_edge = jnp.broadcast_to(cols[:, 3:4], (32, 128))
        first_left = face_flux(r_edge, r[:, :128], p_edge, p[:, :128])[:, 0:1]
        left = jnp.where(lane == 0, first_left, pltpu.roll(right, 1, 1))
        change = TIME_STEP * ((above - below) + (right - left))
        new_out[32 * block : 32 * block + 32, :] = 0.5 * (r - change)
    new_store = pltpu.make_async_copy(new_out, new_ref, load_sem.at[3])
    new_store.start()

    for p in range(6):
        for c in range(2):
            sent(p, c)
    for which in range(2):
        for kind in range(2):
            for k in range(2):
                halo(which, kind, k).wait_send()
    weights_first.wait_send()
    weights_second.wait_send()

    @pl.when(row_moves)
    def _():
        row_first.wait_send()

    @pl.when(lower)
    def _():
        row_second.wait_send()

    pot_store.wait()
    new_store.wait()


def local(density, kernel_hat):
    constants, index = flat_constants()
    pieces, packs = pack(constants)
    vmem = lambda *shape: pltpu.VMEM(shape, F32)
    dma = lambda *shape: pltpu.SemaphoreType.DMA(shape)
    n_const = len(constants)
    scratch = [pltpu.VMEM(c.shape, c.dtype) for c in constants] + [
        vmem(ROWS, COLS), vmem(16, N), vmem(8, N), vmem(512, 128), vmem(512, 128), vmem(1, N), vmem(1, N), vmem(1, N), vmem(8, N),
        vmem(512, 128), vmem(512, 128), vmem(512, 256), vmem(512, 256),
        vmem(2, 32, 8, 256), vmem(2, 32, 8, 256),
        vmem(2, 512, 128), vmem(2, 512, 128), vmem(2, 512, 128), vmem(2, 512, 128),
        vmem(2, 512, 128), vmem(2, 512, 128), vmem(2, 512, 128), vmem(2, 512, 128),
        vmem(2, 256, 256), vmem(512, 256),
        vmem(4, 1, COLS), vmem(4, 1, ROWS), vmem(4, 1, COLS), vmem(4, 1, ROWS),
        vmem(ROWS + 16, COLS), vmem(ROWS + 16, COLS), vmem(ROWS, COLS), vmem(ROWS, COLS),
        dma(6, 2), dma(6, 2, 2), dma(6, 2, 2), dma(4), dma(len(pieces)), dma(4), dma(4), dma(8), dma(8),
    ]
    out = jax.ShapeDtypeStruct((ROWS, COLS), F32)
    half_potential, half_density = pl.pallas_call(
        functools.partial(kernel, index, n_const, pieces),
        out_shape=(out, out),
        in_specs=[pl.BlockSpec(memory_space=pl.ANY)] * 4,
        out_specs=(pl.BlockSpec(memory_space=pl.ANY),) * 2,
        scratch_shapes=scratch,
        compiler_params=pltpu.CompilerParams(
            collective_id=0, has_side_effects=True, vmem_limit_bytes=52 * 1024 * 1024
        ),
        name="convolve_step",
    )(density, kernel_hat, *[jnp.asarray(p) for p in packs])
    return 2.0 * half_potential, 2.0 * half_density


def solution(mesh):
    return jax.shard_map(
        local, mesh=mesh, in_specs=(P("gx", "gy"), P(("gx", "gy"), None)),
        out_specs=(P("gx", "gy"), P("gx", "gy")), check_vma=False,
    )
```
